256 devices in a mesh: ctx: 16 (over y, x), head: 8 (over z_lo, core), pool: 2 (over z_hi).
Axes of the slice: x: 4, y: 4, z: 8 (z_hi: 2, z_lo: 4; z = z_hi * 4 + z_lo), core: 2. Of those that a mesh axis runs over, the one named last changes fastest.
Arguments:
- queries: bfloat16 [256, 64, 128], P(None, 'head'), may hold values from -200 to 200
- prefix_keys: bfloat16 [8192, 8, 128], P(('ctx', 'pool'), 'head'), may hold values from -6 to 6
- prefix_values: bfloat16 [8192, 8, 128], P(('ctx', 'pool'), 'head'), may hold values from -6 to 6
- new_states: bfloat16 [1536, 8192], P(None, ('ctx', 'pool')), may hold values from -7 to 7
- key_weight: bfloat16 [8192, 1024], P(('ctx', 'pool'), 'head'), may hold values from -0.0625 to 0.0625
- value_weight: bfloat16 [8192, 1024], P(('ctx', 'pool'), 'head'), may hold values from -0.0625 to 0.0625
- suffix_keys: bfloat16 [32, 256, 8, 128], P(('ctx', 'pool'), None, 'head'), may hold values from -8 to 8
- suffix_values: bfloat16 [32, 256, 8, 128], P(('ctx', 'pool'), None, 'head'), may hold values from -6 to 6
- suffix_lengths: int32 [32], P(('ctx', 'pool')), may hold values from 1 to 256
- assignment: int32 [256], replicated, may hold values from 0 to 31
- out_weight: bfloat16 [8192, 8192], P('head', ('ctx', 'pool')), may hold values from -0.25 to 0.25
Outputs:
- projected: bfloat16 [256, 8192], P('head', ('ctx', 'pool'))
- new_keys: bfloat16 [1536, 8, 128], P(('ctx', 'pool'), 'head')
- new_values: bfloat16 [1536, 8, 128], P(('ctx', 'pool'), 'head')
The draws below stay inside these ranges and needn't reach their ends.
All inputs are finite; a program needn't handle non-finite values.
Results may differ from the reference program's by a relative error of at most 0.0102.
Values may be sent and summed in bfloat16 or wider, within the bound.
A program may use at most 64 MiB of HBM per device.

```python
import math
import jax
import jax.numpy as jnp
from jax import lax

D = 8192
HQ = 64
KVH = 8
HD = 128
PART = 256
SLEN = 256
PREFIX = 8192
NEW = 1536
SUF = 32


def shared_draw(key):
    base_key = jax.random.fold_in(key, 7)
    key_one, key_two = jax.random.split(base_key, 2)
    cached = jnp.clip(jax.random.normal(key_one, (PREFIX, KVH, HD), jnp.float32), -6.0, 6.0)
    asked = jnp.clip(2.5 * jax.random.normal(key_two, (PART, HQ, HD), jnp.float32), -15.0, 15.0)
    return (asked, cached)


def draw_queries(key, part):
    return shared_draw(key)[0].astype(jnp.bfloat16)


def draw_prefix_keys(key, part):
    return shared_draw(key)[1].astype(jnp.bfloat16)


def plant(entries, rng, least, high):
    extent = entries.shape
    index_at = [jax.random.randint(jax.random.fold_in(rng, axis), (), 0, extent[axis]) for axis in range(len(extent))]
    entries = entries.at[tuple(index_at)].set(least)
    longest = extent.index(max(extent))
    index_at[longest] = (index_at[longest] + 1) % extent[longest]
    return entries.at[tuple(index_at)].set(high)


def levels(key, extent, shards, low, top_value):
    factor_of, own = 1.0, jax.random.fold_in(key, 6)
    for dim, shards_of in shards:
        steps = jnp.exp(jax.random.uniform(jax.random.fold_in(own, dim), (shards_of,), jnp.float32, low / len(shards), top_value / len(shards)))
        factor_of = factor_of * jnp.repeat(steps, extent[dim] // shards_of).reshape([-1 if axis == dim else 1 for axis in range(len(extent))])
    return factor_of


def normal_values(key, extent, scale, reach, cuts=(), kind=jnp.bfloat16):
    values = jax.random.normal(key, extent, jnp.float32) * scale
    if len(cuts) > 0:
        values = levels(key, extent, cuts, -0.22, 0.18) * values
    return jnp.clip(values, min=-reach, max=reach).astype(kind)


def setup_inputs(seed: int = 0) -> dict:
    keys = jax.random.split(jax.random.key(seed), 12)
    queries = draw_queries(jax.random.fold_in(keys[11], 71), 0)
    prefix_keys = draw_prefix_keys(jax.random.fold_in(keys[11], 71), 0)
    prefix_values = normal_values(keys[2], (PREFIX, KVH, HD), 1.0, 6.0, ((0, 32), (1, 8)))
    new_states = normal_values(keys[3], (NEW, D), 1.2, 7.0, ((1, 32),))
    key_weight = normal_values(keys[4], (D, KVH * HD), D ** -0.5, 0.0625, ((0, 32), (1, 8)))
    value_weight = normal_values(keys[5], (D, KVH * HD), D ** -0.5, 0.0625, ((0, 32), (1, 8)))
    suffix_keys = normal_values(keys[6], (SUF, SLEN, KVH, HD), 1.4, 8.0, ((0, 32), (2, 8)))
    suffix_values = normal_values(keys[7], (SUF, SLEN, KVH, HD), 1.0, 6.0, ((0, 32), (2, 8)))
    suffix_lengths = plant(jax.random.randint(keys[8], (SUF,), 1, SLEN + 1), jax.random.fold_in(keys[8], 1), 1, SLEN).astype(jnp.int32)
    assignment = plant(jax.random.randint(keys[9], (PART,), 0, SUF), jax.random.fold_in(keys[9], 1), 0, SUF - 1).astype(jnp.int32)
    out_weight = normal_values(keys[10], (HQ * HD, D), (D // 16) ** -0.5, 0.25, ((0, 8), (1, 32)))
    return dict(queries=queries, prefix_keys=prefix_keys, prefix_values=prefix_values, new_states=new_states, key_weight=key_weight, value_weight=value_weight, suffix_keys=suffix_keys, suffix_values=suffix_values, suffix_lengths=suffix_lengths, assignment=assignment, out_weight=out_weight)


def rotate(values, positions):
    half_dim = values.shape[-1] // 2
    frequency = jnp.exp(jnp.arange(half_dim, dtype=jnp.float32) * (-2.0 * math.log(500000.0) / values.shape[-1]))
    angles = positions.astype(jnp.float32)[:, None] * frequency[None, :]
    cosine = jnp.cos(angles)[:, None, :]
    sine_part = jnp.sin(angles)[:, None, :]
    front = values[..., :half_dim]
    second = values[..., half_dim:]
    return jnp.concatenate([front * cosine - second * sine_part, second * cosine + front * sine_part], -1)


def attend_group(group_queries, group_keys, group_values, chosen_keys, chosen_values, usable):
    group_size = group_queries.shape[1]
    key_count = group_keys.shape[0]
    block_rows = math.gcd(PART, 128)
    block_count = PART // block_rows
    inv_scale = HD ** -0.5

    def one_block(inputs):
        block_q, block_k, block_v, block_use = inputs
        query_rows = block_q.reshape(block_rows * group_size, HD)
        main_scores = jnp.dot(query_rows, group_keys.T, preferred_element_type=jnp.float32) * inv_scale
        main_scores = main_scores.reshape(block_rows, group_size, key_count)
        side_scores = jnp.einsum("pgd,psd->pgs", block_q.astype(jnp.float32), block_k.astype(jnp.float32)) * inv_scale
        side_scores = jnp.where(block_use[:, None, :], side_scores, -jnp.inf)
        maxima = jnp.maximum(jnp.max(main_scores, -1), jnp.max(side_scores, -1))
        main_exp = jnp.exp(main_scores - maxima[..., None])
        side_exp = jnp.exp(side_scores - maxima[..., None])
        totals = jnp.sum(main_exp, -1) + jnp.sum(side_exp, -1)
        main_part = jnp.dot(main_exp.astype(jnp.bfloat16).reshape(block_rows * group_size, key_count), group_values, preferred_element_type=jnp.float32)
        side_part = jnp.einsum("pgs,psd->pgd", side_exp.astype(jnp.bfloat16).astype(jnp.float32), block_v.astype(jnp.float32))
        weighted = main_part.reshape(block_rows, group_size, HD) + side_part
        return (weighted / totals[..., None]).astype(jnp.bfloat16)

    inputs = (group_queries.reshape(block_count, block_rows, group_size, HD),
              chosen_keys.reshape(block_count, block_rows, SLEN, HD),
              chosen_values.reshape(block_count, block_rows, SLEN, HD),
              usable.reshape(block_count, block_rows, SLEN))
    return lax.map(one_block, inputs).reshape(PART, group_size, HD)


def reference(queries, prefix_keys, prefix_values, new_states, key_weight, value_weight, suffix_keys, suffix_values, suffix_lengths, assignment, out_weight):
    group_size = HQ // KVH
    raw_keys = jnp.dot(new_states, key_weight, preferred_element_type=jnp.float32).reshape(NEW, KVH, HD)
    positions = PREFIX + jnp.arange(NEW, dtype=jnp.int32)
    new_keys = rotate(raw_keys, positions).astype(jnp.bfloat16)
    new_values = jnp.dot(new_states, value_weight, preferred_element_type=jnp.float32).reshape(NEW, KVH, HD).astype(jnp.bfloat16)
    keys_all = jnp.concatenate([prefix_keys, new_keys], 0).transpose(1, 0, 2)
    values_all = jnp.concatenate([prefix_values, new_values], 0).transpose(1, 0, 2)
    query_groups = queries.reshape(PART, KVH, group_size, HD).transpose(1, 0, 2, 3)
    usable = jnp.arange(SLEN, dtype=jnp.int32)[None, :] < suffix_lengths[assignment][:, None]

    def per_group(inputs):
        group_queries, group_keys, group_values, side_keys, side_values = inputs
        return attend_group(group_queries, group_keys, group_values, side_keys[assignment], side_values[assignment], usable)

    attention = lax.map(per_group, (query_groups, keys_all, values_all, suffix_keys.transpose(2, 0, 1, 3), suffix_values.transpose(2, 0, 1, 3)))
    attention = attention.transpose(1, 0, 2, 3).reshape(PART, HQ * HD)
    projected = jnp.dot(attention, out_weight, preferred_element_type=jnp.float32).astype(jnp.bfloat16)
    return (projected, new_keys, new_values)
```

```python
import functools
import math

import jax
import jax.numpy as jnp
import numpy as np
from jax import lax
from jax.experimental import pallas as pl
from jax.experimental.pallas import tpu as pltpu
from jax.sharding import PartitionSpec as P

F32 = jnp.float32
BF16 = jnp.bfloat16
NX = 4
PLANE = 16
POOL = 2
HEADS = 8
GROUP = 8
HD = 128
PREFIX = 8192
NEW = 1536
NEW_DEV = NEW // (PLANE * POOL)
NEW_CHIP = NEW_DEV * POOL
FEAT = 256
ROWS = 2048
CHUNK = 128
CACHED = 256
SUFFIX = 256
MSG = HD + 16
OUT_COLS = 256
SCALE = HD**-0.5


def rotary_tables():
    half = HD // 2
    frequency = np.exp(
        np.arange(half, dtype=np.float32) * np.float32(-2.0 * math.log(500000.0) / HD)
    ).astype(np.float32)
    positions = (PREFIX + np.arange(NEW)).astype(np.float32)
    angles = (positions[:, None] * frequency[None, :]).astype(np.float32).astype(np.float64)
    cosine = np.cos(angles).astype(np.float32)
    sine = np.sin(angles).astype(np.float32)
    both = np.concatenate([cosine, cosine, -sine, sine], 1)
    return both.reshape(PLANE * POOL, NEW_DEV, 2 * HD)


def mm(a, b, ca, cb):
    return lax.dot_general(a, b, (((ca,), (cb,)), ((), ())), preferred_element_type=F32)


def stat_rows(m, l):
    m1 = m.astype(BF16).astype(F32)
    r = m - m1
    m2 = r.astype(BF16).astype(F32)
    m3 = r - m2
    l1 = l.astype(BF16).astype(F32)
    r = l - l1
    l2 = r.astype(BF16).astype(F32)
    l3 = r - l2
    row = lax.broadcasted_iota(jnp.int32, (16, CHUNK), 0)
    out = jnp.zeros((16, CHUNK), F32)
    for k, part in enumerate((m1, m2, m3, l1, l2, l3)):
        out = jnp.where(row == k, jnp.broadcast_to(part, (16, CHUNK)), out)
    return out.astype(BF16)


def read_stats(tile):
    t = tile.astype(F32)
    m = (t[0:1] + t[1:2]) + t[2:3]
    l = (t[3:4] + t[4:5]) + t[5:6]
    return m, l


def kernel(
    q_hbm, pk_hbm, pv_hbm, st_hbm, kw_hbm, vw_hbm, sk_hbm, sv_hbm, len_ref, asg_ref, ow_hbm, rot_hbm,
    proj_ref, nk_ref, nv_ref,
    st_v, w_v, q_v, k_v, v_v, vt_v, ow_v, rot_v,
    kv_send, kv_recv, kvz_send, kvz_recv,
    acc_v, m_v, l_v,
    att_send, att_recv, attz_send, attz_recv,
    ag_v, part_v, out_send, out_recv,
    lsem, s1, r1, s2, r2, s3, r3, s4, r4, s5, r5, s6, r6,
):
    c = lax.axis_index("ctx")
    h = lax.axis_index("head")
    p = lax.axis_index("pool")
    y = c // NX
    x = c % NX

    def plane_peer(i):
        return ((y + i // NX) % NX) * NX + (x + i % NX) % NX

    def remote(src, dst, ss, rs, cc, hh, pp):
        return pltpu.make_async_remote_copy(
            src_ref=src, dst_ref=dst, send_sem=ss, recv_sem=rs,
            device_id={"ctx": cc, "head": hh, "pool": pp},
            device_id_type=pl.DeviceIdType.MESH,
        )

    barrier = pltpu.get_barrier_semaphore()

    def greet(i, carry):
        pl.semaphore_signal(
            barrier, inc=1, device_id={"ctx": plane_peer(i), "head": h, "pool": p},
            device_id_type=pl.DeviceIdType.MESH,
        )
        return carry

    lax.fori_loop(1, PLANE, greet, 0)
    pl.semaphore_signal(
        barrier, inc=1, device_id={"ctx": c, "head": h, "pool": 1 - p},
        device_id_type=pl.DeviceIdType.MESH,
    )

    def greet_head(j, carry):
        pl.semaphore_signal(
            barrier, inc=1, device_id={"ctx": c, "head": (h + j) % HEADS, "pool": p},
            device_id_type=pl.DeviceIdType.MESH,
        )
        return carry

    lax.fori_loop(1, HEADS, greet_head, 0)

    shard = c * POOL + p
    loads = [
        pltpu.make_async_copy(st_hbm, st_v, lsem.at[0]),
        pltpu.make_async_copy(kw_hbm, w_v.at[:, pl.ds(0, HD)], lsem.at[1]),
        pltpu.make_async_copy(vw_hbm, w_v.at[:, pl.ds(HD, HD)], lsem.at[2]),
        pltpu.make_async_copy(q_hbm, q_v, lsem.at[3]),
        pltpu.make_async_copy(pk_hbm, k_v.at[pl.ds(0, CACHED)], lsem.at[4]),
        pltpu.make_async_copy(sk_hbm, k_v.at[pl.ds(CACHED, SUFFIX)], lsem.at[5]),
        pltpu.make_async_copy(pv_hbm, v_v.at[pl.ds(0, CACHED)], lsem.at[6]),
        pltpu.make_async_copy(sv_hbm, v_v.at[pl.ds(CACHED, SUFFIX)], lsem.at[7]),
        pltpu.make_async_copy(rot_hbm.at[shard], rot_v, lsem.at[8]),
        pltpu.make_async_copy(ow_hbm, ow_v, lsem.at[9]),
    ]
    for copy in loads:
        copy.start()
    for copy in loads[:3]:
        copy.wait()
    pl.semaphore_wait(barrier, (PLANE - 1) + 1 + (HEADS - 1))

    for dy in (2, 1, 3, 0):
        yy = (y + dy) % NX
        first = pl.multiple_of(yy * (NX * NEW_CHIP), NX * NEW_CHIP)
        part = jnp.dot(st_v[pl.ds(first, NX * NEW_CHIP), :], w_v[...], preferred_element_type=F32)
        kv_send[pl.ds(yy * NX, NX)] = part.astype(BF16).reshape(NX, NEW_CHIP, 2 * HD)

        def send_kv(dx, carry, dy=dy, yy=yy):
            i = dy * NX + dx
            cc = yy * NX + (x + dx) % NX
            remote(kv_send.at[cc], kv_recv.at[i], s1.at[i], r1.at[i], cc, h, p).start()
            return carry

        lax.fori_loop(1 if dy == 0 else 0, NX, send_kv, 0)

    for copy in loads[3:8]:
        copy.wait()
    vt_v[...] = v_v[...].astype(F32).T.astype(BF16)
    suffix_id = shard
    lim = jnp.where(asg_ref[...] == suffix_id, len_ref[0], 0).astype(BF16)
    lim = jnp.broadcast_to(lim, (16, 256))

    def cached_block(b, carry):
        who = lax.broadcasted_iota(jnp.int32, (256, 256), 0)
        row = lax.broadcasted_iota(jnp.int32, (256, 256), 1)
        spread = jnp.where(who == b * 32 + row // GROUP, 1.0, 0.0).astype(BF16)
        lim_rows = mm(lim, spread, 1, 0)[0:1]
        qb = q_v[pl.ds(pl.multiple_of(b * 256, 256), 256), :]
        s = mm(k_v[...], qb, 1, 1) * SCALE
        key = lax.broadcasted_iota(jnp.int32, (SUFFIX, 256), 0).astype(F32)
        side = jnp.where(key < lim_rows, s[CACHED:], -jnp.inf)
        m = jnp.maximum(
            jnp.max(s[:CACHED], 0, keepdims=True), jnp.max(side, 0, keepdims=True)
        )
        main_e = jnp.exp(s[:CACHED] - m)
        side_e = jnp.exp(side - m)
        l = jnp.sum(main_e, 0, keepdims=True) + jnp.sum(side_e, 0, keepdims=True)
        e = jnp.concatenate([main_e.astype(BF16), side_e.astype(BF16)], 0)
        o = mm(vt_v[...], e, 1, 0)
        for k in range(2):
            lanes = slice(k * CHUNK, (k + 1) * CHUNK)
            acc_v[b * 2 + k] = o[:, lanes]
            m_v[b * 2 + k] = jnp.broadcast_to(m[:, lanes], (8, CHUNK))
            l_v[b * 2 + k] = jnp.broadcast_to(l[:, lanes], (8, CHUNK))
        return carry

    lax.fori_loop(0, 8, cached_block, 0)

    def sum_kv(i, acc):
        remote(kv_send.at[c], kv_recv.at[i], s1.at[i], r1.at[i], c, h, p).wait_recv()
        return acc + kv_recv[i].astype(F32)

    mine = jnp.dot(
        st_v[pl.ds(pl.multiple_of(c * NEW_CHIP, NEW_CHIP), NEW_CHIP), :], w_v[...],
        preferred_element_type=F32,
    )
    total = lax.fori_loop(1, PLANE, sum_kv, mine)
    low, high = total[:NEW_DEV], total[NEW_DEV:]
    first = p == 0
    kvz_send[...] = jnp.where(first, high, low).astype(BF16)
    swap = remote(kvz_send, kvz_recv, s2, r2, c, h, 1 - p)
    swap.start()
    kept = jnp.where(first, low, high)
    loads[8].wait()
    swap.wait_recv()
    kv = kept + kvz_recv[...].astype(F32)
    raw = kv[:, :HD]
    turned = pltpu.roll(raw, HD // 2, 1)
    new_k = (raw * rot_v[:, :HD] + turned * rot_v[:, HD:]).astype(BF16)
    new_v = kv[:, HD:].astype(BF16)
    nk_ref[...] = new_k
    nv_ref[...] = new_v
    new_vt = new_v.astype(F32).T.astype(BF16)

    def new_block(dy):
        yy = (y + dy) % NX
        qb = q_v[pl.ds(pl.multiple_of(yy * 512, 512), 512), :]
        s = mm(new_k, qb, 1, 1) * SCALE
        s_max = jnp.max(s, 0, keepdims=True)
        for k in range(NX):
            lanes = slice(k * CHUNK, (k + 1) * CHUNK)
            cc = yy * NX + k
            m_old = m_v[cc][0:1]
            m_new = jnp.maximum(m_old, s_max[:, lanes])
            shrink = jnp.exp(m_old - m_new)
            e = jnp.exp(s[:, lanes] - m_new)
            l_new = l_v[cc][0:1] * shrink + jnp.sum(e, 0, keepdims=True)
            o = acc_v[cc] * shrink + mm(new_vt, e.astype(BF16), 1, 0)
            att_send[cc, 0:HD] = o.astype(BF16)
            att_send[cc, HD:MSG] = stat_rows(m_new, l_new)
            if dy == 0:
                acc_v[cc] = o
                m_v[cc] = jnp.broadcast_to(m_new, (8, CHUNK))
                l_v[cc] = jnp.broadcast_to(l_new, (8, CHUNK))

    for dy in (2, 1, 3, 0):
        new_block(dy)

        def send_att(dx, carry, dy=dy):
            i = dy * NX + dx
            cc = ((y + dy) % NX) * NX + (x + dx) % NX
            remote(att_send.at[cc], att_recv.at[i], s3.at[i], r3.at[i], cc, h, p).start()
            return carry

        lax.fori_loop(1 if dy == 0 else 0, NX, send_att, 0)

    def merge(state, block):
        acc, m, l = state
        m_in, l_in = read_stats(block[HD:MSG])
        m_all = jnp.maximum(m, m_in)
        a = jnp.exp(m - m_all)
        b = jnp.exp(m_in - m_all)
        return (acc * a + block[0:HD].astype(F32) * b, m_all, l * a + l_in * b)

    def sum_att(i, state):
        remote(att_send.at[c], att_recv.at[i], s3.at[i], r3.at[i], c, h, p).wait_recv()
        return merge(state, att_recv[i])

    state = lax.fori_loop(1, PLANE, sum_att, (acc_v[c], m_v[c][0:1], l_v[c][0:1]))
    attz_send[0:HD] = state[0].astype(BF16)
    attz_send[HD:MSG] = stat_rows(state[1], state[2])
    swap_att = remote(attz_send, attz_recv, s4, r4, c, h, 1 - p)
    swap_att.start()
    swap_att.wait_recv()
    acc, _, l = merge(state, attz_recv[...])
    att = (acc / l).astype(BF16)
    to = lax.broadcasted_iota(jnp.int32, (CHUNK, CHUNK), 0)
    frm = lax.broadcasted_iota(jnp.int32, (CHUNK, CHUNK), 1)
    perm = jnp.where(frm == (to % 16) * GROUP + to // 16, 1.0, 0.0).astype(BF16)
    ag_v[c] = mm(perm, att, 1, 1).astype(BF16)

    def send_ag(i, carry):
        remote(ag_v.at[c], ag_v.at[c], s5.at[i], r5.at[i], plane_peer(i), h, p).start()
        return carry

    lax.fori_loop(1, PLANE, send_ag, 0)
    loads[9].wait()

    def wait_ag(i, carry):
        src = ((y + NX - i // NX) % NX) * NX + (x + NX - i % NX) % NX
        remote(ag_v.at[c], ag_v.at[src], s5.at[i], r5.at[i], c, h, p).wait_recv()
        return carry

    lax.fori_loop(1, PLANE, wait_ag, 0)

    out = jnp.zeros((256, OUT_COLS), F32)
    for g in range(GROUP):
        a = ag_v[:, g * 16:(g + 1) * 16, :].reshape(256, HD)
        out = out + jnp.dot(a, ow_v[g * HD:(g + 1) * HD, :], preferred_element_type=F32)
    part_v[...] = out.reshape(HEADS, 32, OUT_COLS)
    out_send[...] = out.astype(BF16).reshape(HEADS, 32, OUT_COLS)

    def send_out(j, carry):
        hh = (h + j) % HEADS
        remote(out_send.at[hh], out_recv.at[j], s6.at[j], r6.at[j], c, hh, p).start()
        return carry

    lax.fori_loop(1, HEADS, send_out, 0)

    def sum_out(j, acc):
        remote(out_send.at[h], out_recv.at[j], s6.at[j], r6.at[j], c, h, p).wait_recv()
        return acc + out_recv[j].astype(F32)

    proj_ref[...] = lax.fori_loop(1, HEADS, sum_out, part_v[h]).astype(BF16)

    def drain(i, carry):
        remote(kv_send.at[c], kv_recv.at[i], s1.at[i], r1.at[i], c, h, p).wait_send()
        remote(att_send.at[c], att_recv.at[i], s3.at[i], r3.at[i], c, h, p).wait_send()
        remote(ag_v.at[c], ag_v.at[c], s5.at[i], r5.at[i], c, h, p).wait_send()
        return carry

    lax.fori_loop(1, PLANE, drain, 0)
    swap.wait_send()
    swap_att.wait_send()

    def drain_out(j, carry):
        remote(out_send.at[h], out_recv.at[j], s6.at[j], r6.at[j], c, h, p).wait_send()
        return carry

    lax.fori_loop(1, HEADS, drain_out, 0)


def body(
    queries, prefix_keys, prefix_values, new_states, key_weight, value_weight,
    suffix_keys, suffix_values, suffix_lengths, assignment, out_weight,
):
    rot = jnp.asarray(rotary_tables())
    hbm = pl.BlockSpec(memory_space=pl.ANY)
    vmem = pl.BlockSpec(memory_space=pltpu.VMEM)
    smem = pl.BlockSpec(memory_space=pltpu.SMEM)
    dma = pltpu.SemaphoreType.DMA
    projected, new_keys, new_values = pl.pallas_call(
        kernel,
        out_shape=(
            jax.ShapeDtypeStruct((32, OUT_COLS), BF16),
            jax.ShapeDtypeStruct((NEW_DEV, HD), BF16),
            jax.ShapeDtypeStruct((NEW_DEV, HD), BF16),
        ),
        in_specs=[hbm] * 8 + [smem, vmem, hbm, hbm],
        out_specs=(vmem, vmem, vmem),
        scratch_shapes=[
            pltpu.VMEM((NEW, FEAT), BF16),
            pltpu.VMEM((FEAT, 2 * HD), BF16),
            pltpu.VMEM((ROWS, HD), BF16),
            pltpu.VMEM((CACHED + SUFFIX, HD), BF16),
            pltpu.VMEM((CACHED + SUFFIX, HD), BF16),
            pltpu.VMEM((HD, CACHED + SUFFIX), BF16),
            pltpu.VMEM((GROUP * HD, OUT_COLS), BF16),
            pltpu.VMEM((NEW_DEV, 2 * HD), F32),
            pltpu.VMEM((PLANE, NEW_CHIP, 2 * HD), BF16),
            pltpu.VMEM((PLANE, NEW_CHIP, 2 * HD), BF16),
            pltpu.VMEM((NEW_DEV, 2 * HD), BF16),
            pltpu.VMEM((NEW_DEV, 2 * HD), BF16),
            pltpu.VMEM((PLANE, HD, CHUNK), F32),
            pltpu.VMEM((PLANE, 8, CHUNK), F32),
            pltpu.VMEM((PLANE, 8, CHUNK), F32),
            pltpu.VMEM((PLANE, MSG, CHUNK), BF16),
            pltpu.VMEM((PLANE, MSG, CHUNK), BF16),
            pltpu.VMEM((MSG, CHUNK), BF16),
            pltpu.VMEM((MSG, CHUNK), BF16),
            pltpu.VMEM((PLANE, CHUNK, HD), BF16),
            pltpu.VMEM((HEADS, 32, OUT_COLS), F32),
            pltpu.VMEM((HEADS, 32, OUT_COLS), BF16),
            pltpu.VMEM((HEADS, 32, OUT_COLS), BF16),
            dma((10,)),
            dma((PLANE,)), dma((PLANE,)),
            dma, dma,
            dma((PLANE,)), dma((PLANE,)),
            dma, dma,
            dma((PLANE,)), dma((PLANE,)),
            dma((HEADS,)), dma((HEADS,)),
        ],
        compiler_params=pltpu.CompilerParams(
            collective_id=0, has_side_effects=True, vmem_limit_bytes=40 * 1024 * 1024
        ),
    )(
        queries.reshape(ROWS, HD),
        prefix_keys.reshape(CACHED, HD),
        prefix_values.reshape(CACHED, HD),
        new_states,
        key_weight,
        value_weight,
        suffix_keys.reshape(SUFFIX, HD),
        suffix_values.reshape(SUFFIX, HD),
        suffix_lengths,
        assignment.reshape(1, 256),
        out_weight,
        rot,
    )
    return (
        projected,
        new_keys.reshape(NEW_DEV, 1, HD),
        new_values.reshape(NEW_DEV, 1, HD),
    )


def solution(mesh):
    in_specs = (
        P(None, "head", None),
        P(("ctx", "pool"), "head", None),
        P(("ctx", "pool"), "head", None),
        P(None, ("ctx", "pool")),
        P(("ctx", "pool"), "head"),
        P(("ctx", "pool"), "head"),
        P(("ctx", "pool"), None, "head", None),
        P(("ctx", "pool"), None, "head", None),
        P(("ctx", "pool")),
        P(),
        P("head", ("ctx", "pool")),
    )
    out_specs = (
        P("head", ("ctx", "pool")),
        P(("ctx", "pool"), "head", None),
        P(("ctx", "pool"), "head", None),
    )
    return jax.shard_map(body, mesh=mesh, in_specs=in_specs, out_specs=out_specs, check_vma=False)
```

```python
import functools
import math

import jax
import jax.numpy as jnp
import numpy as np
from jax import lax
from jax.experimental import pallas as pl
from jax.experimental.pallas import tpu as pltpu
from jax.sharding import PartitionSpec as P

F32 = jnp.float32
BF16 = jnp.bfloat16
NX = 4
PLANE = 16
POOL = 2
HEADS = 8
GROUP = 8
HD = 128
PREFIX = 8192
NEW = 1536
NEW_DEV = NEW // (PLANE * POOL)
NEW_CHIP = NEW_DEV * POOL
FEAT = 256
ROWS = 2048
CHUNK = 128
CACHED = 256
SUFFIX = 256
MSG = HD + 16
OUT_COLS = 256
SCALE = HD**-0.5


def rotary_tables():
    half = HD // 2
    frequency = np.exp(
        np.arange(half, dtype=np.float32) * np.float32(-2.0 * math.log(500000.0) / HD)
    ).astype(np.float32)
    positions = (PREFIX + np.arange(NEW)).astype(np.float32)
    angles = (positions[:, None] * frequency[None, :]).astype(np.float32).astype(np.float64)
    cosine = np.cos(angles).astype(np.float32)
    sine = np.sin(angles).astype(np.float32)
    both = np.concatenate([cosine, cosine, -sine, sine], 1)
    return both.reshape(PLANE * POOL, NEW_DEV, 2 * HD)


def mm(a, b, ca, cb):
    return lax.dot_general(a, b, (((ca,), (cb,)), ((), ())), preferred_element_type=F32)


def stat_rows(m, l):
    m1 = m.astype(BF16).astype(F32)
    r = m - m1
    m2 = r.astype(BF16).astype(F32)
    m3 = r - m2
    l1 = l.astype(BF16).astype(F32)
    r = l - l1
    l2 = r.astype(BF16).astype(F32)
    l3 = r - l2
    row = lax.broadcasted_iota(jnp.int32, (16, CHUNK), 0)
    out = jnp.zeros((16, CHUNK), F32)
    for k, part in enumerate((m1, m2, m3, l1, l2, l3)):
        out = jnp.where(row == k, jnp.broadcast_to(part, (16, CHUNK)), out)
    return out.astype(BF16)


def read_stats(tile):
    t = tile.astype(F32)
    m = (t[0:1] + t[1:2]) + t[2:3]
    l = (t[3:4] + t[4:5]) + t[5:6]
    return m, l


def kernel(
    q_hbm, pk_hbm, pv_hbm, st_hbm, kw_hbm, vw_hbm, sk_hbm, sv_hbm, len_hbm, asg_hbm, ow_hbm, rot_hbm,
    proj_ref, nk_ref, nv_ref,
    st_v, w_v, q_v, k_v, v_v, vt_v, ow_v, rot_v, len_v, asg_v,
    kv_send, kv_recv, kvz_send, kvz_recv,
    acc_v, m_v, l_v,
    att_send, att_recv, attz_send, attz_recv,
    ag_v, part_v, out_send, out_recv,
    lsem, s1, r1, s2, r2, s3, r3, s4, r4, s5, r5, s6, r6,
):
    c = lax.axis_index("ctx")
    h = lax.axis_index("head")
    p = lax.axis_index("pool")
    y = c // NX
    x = c % NX

    def plane_peer(i):
        return ((y + i // NX) % NX) * NX + (x + i % NX) % NX

    def remote(src, dst, ss, rs, cc, hh, pp):
        return pltpu.make_async_remote_copy(
            src_ref=src, dst_ref=dst, send_sem=ss, recv_sem=rs,
            device_id={"ctx": cc, "head": hh, "pool": pp},
            device_id_type=pl.DeviceIdType.MESH,
        )

    barrier = pltpu.get_barrier_semaphore()

    def greet(i, carry):
        pl.semaphore_signal(
            barrier, inc=1, device_id={"ctx": plane_peer(i), "head": h, "pool": p},
            device_id_type=pl.DeviceIdType.MESH,
        )
        return carry

    lax.fori_loop(1, PLANE, greet, 0)
    pl.semaphore_signal(
        barrier, inc=1, device_id={"ctx": c, "head": h, "pool": 1 - p},
        device_id_type=pl.DeviceIdType.MESH,
    )

    def greet_head(j, carry):
        pl.semaphore_signal(
            barrier, inc=1, device_id={"ctx": c, "head": (h + j) % HEADS, "pool": p},
            device_id_type=pl.DeviceIdType.MESH,
        )
        return carry

    lax.fori_loop(1, HEADS, greet_head, 0)

    shard = c * POOL + p
    loads = [
        pltpu.make_async_copy(st_hbm, st_v, lsem.at[0]),
        pltpu.make_async_copy(kw_hbm, w_v.at[:, pl.ds(0, HD)], lsem.at[1]),
        pltpu.make_async_copy(vw_hbm, w_v.at[:, pl.ds(HD, HD)], lsem.at[2]),
        pltpu.make_async_copy(q_hbm, q_v, lsem.at[3]),
        pltpu.make_async_copy(pk_hbm, k_v.at[pl.ds(0, CACHED)], lsem.at[4]),
        pltpu.make_async_copy(sk_hbm, k_v.at[pl.ds(CACHED, SUFFIX)], lsem.at[5]),
        pltpu.make_async_copy(pv_hbm, v_v.at[pl.ds(0, CACHED)], lsem.at[6]),
        pltpu.make_async_copy(sv_hbm, v_v.at[pl.ds(CACHED, SUFFIX)], lsem.at[7]),
        pltpu.make_async_copy(rot_hbm.at[shard], rot_v, lsem.at[8]),
        pltpu.make_async_copy(ow_hbm, ow_v, lsem.at[9]),
        pltpu.make_async_copy(len_hbm, len_v, lsem.at[10]),
        pltpu.make_async_copy(asg_hbm, asg_v, lsem.at[11]),
    ]
    for copy in loads:
        copy.start()
    for copy in loads[:3]:
        copy.wait()
    pl.semaphore_wait(barrier, (PLANE - 1) + 1 + (HEADS - 1))

    for dy in (2, 1, 3, 0):
        yy = (y + dy) % NX
        first = pl.multiple_of(yy * (NX * NEW_CHIP), NX * NEW_CHIP)
        part = jnp.dot(st_v[pl.ds(first, NX * NEW_CHIP), :], w_v[...], preferred_element_type=F32)
        kv_send[pl.ds(yy * NX, NX)] = part.astype(BF16).reshape(NX, NEW_CHIP, 2 * HD)

        def send_kv(dx, carry, dy=dy, yy=yy):
            i = dy * NX + dx
            cc = yy * NX + (x + dx) % NX
            remote(kv_send.at[cc], kv_recv.at[i], s1.at[i], r1.at[i], cc, h, p).start()
            return carry

        lax.fori_loop(1 if dy == 0 else 0, NX, send_kv, 0)

    for copy in loads[3:8] + loads[10:]:
        copy.wait()
    vt_v[...] = v_v[...].astype(F32).T.astype(BF16)
    suffix_id = shard
    lim = jnp.where(asg_v[...] == suffix_id, len_v[0], 0).astype(BF16)
    lim = jnp.broadcast_to(lim, (16, 256))

    def cached_block(b, carry):
        who = lax.broadcasted_iota(jnp.int32, (256, 256), 0)
        row = lax.broadcasted_iota(jnp.int32, (256, 256), 1)
        spread = jnp.where(who == b * 32 + row // GROUP, 1.0, 0.0).astype(BF16)
        lim_rows = mm(lim, spread, 1, 0)[0:1]
        qb = q_v[pl.ds(pl.multiple_of(b * 256, 256), 256), :]
        s = mm(k_v[...], qb, 1, 1) * SCALE
        key = lax.broadcasted_iota(jnp.int32, (SUFFIX, 256), 0).astype(F32)
        side = jnp.where(key < lim_rows, s[CACHED:], -jnp.inf)
        m = jnp.maximum(
            jnp.max(s[:CACHED], 0, keepdims=True), jnp.max(side, 0, keepdims=True)
        )
        main_e = jnp.exp(s[:CACHED] - m)
        side_e = jnp.exp(side - m)
        l = jnp.sum(main_e, 0, keepdims=True) + jnp.sum(side_e, 0, keepdims=True)
        e = jnp.concatenate([main_e.astype(BF16), side_e.astype(BF16)], 0)
        o = mm(vt_v[...], e, 1, 0)
        for k in range(2):
            lanes = slice(k * CHUNK, (k + 1) * CHUNK)
            acc_v[b * 2 + k] = o[:, lanes]
            m_v[b * 2 + k] = jnp.broadcast_to(m[:, lanes], (8, CHUNK))
            l_v[b * 2 + k] = jnp.broadcast_to(l[:, lanes], (8, CHUNK))
        return carry

    lax.fori_loop(0, 8, cached_block, 0)

    def sum_kv(i, acc):
        remote(kv_send.at[c], kv_recv.at[i], s1.at[i], r1.at[i], c, h, p).wait_recv()
        return acc + kv_recv[i].astype(F32)

    mine = jnp.dot(
        st_v[pl.ds(pl.multiple_of(c * NEW_CHIP, NEW_CHIP), NEW_CHIP), :], w_v[...],
        preferred_element_type=F32,
    )
    total = lax.fori_loop(1, PLANE, sum_kv, mine)
    low, high = total[:NEW_DEV], total[NEW_DEV:]
    first = p == 0
    kvz_send[...] = jnp.where(first, high, low).astype(BF16)
    swap = remote(kvz_send, kvz_recv, s2, r2, c, h, 1 - p)
    swap.start()
    kept = jnp.where(first, low, high)
    loads[8].wait()
    swap.wait_recv()
    kv = kept + kvz_recv[...].astype(F32)
    raw = kv[:, :HD]
    turned = pltpu.roll(raw, HD // 2, 1)
    new_k = (raw * rot_v[:, :HD] + turned * rot_v[:, HD:]).astype(BF16)
    new_v = kv[:, HD:].astype(BF16)
    nk_ref[...] = new_k
    nv_ref[...] = new_v
    new_vt = new_v.astype(F32).T.astype(BF16)

    def new_block(dy):
        yy = (y + dy) % NX
        qb = q_v[pl.ds(pl.multiple_of(yy * 512, 512), 512), :]
        s = mm(new_k, qb, 1, 1) * SCALE
        s_max = jnp.max(s, 0, keepdims=True)
        for k in range(NX):
            lanes = slice(k * CHUNK, (k + 1) * CHUNK)
            cc = yy * NX + k
            m_old = m_v[cc][0:1]
            m_new = jnp.maximum(m_old, s_max[:, lanes])
            shrink = jnp.exp(m_old - m_new)
            e = jnp.exp(s[:, lanes] - m_new)
            l_new = l_v[cc][0:1] * shrink + jnp.sum(e, 0, keepdims=True)
            o = acc_v[cc] * shrink + mm(new_vt, e.astype(BF16), 1, 0)
            att_send[cc, 0:HD] = o.astype(BF16)
            att_send[cc, HD:MSG] = stat_rows(m_new, l_new)
            if dy == 0:
                acc_v[cc] = o
                m_v[cc] = jnp.broadcast_to(m_new, (8, CHUNK))
                l_v[cc] = jnp.broadcast_to(l_new, (8, CHUNK))

    for dy in (2, 1, 3, 0):
        new_block(dy)

        def send_att(dx, carry, dy=dy):
            i = dy * NX + dx
            cc = ((y + dy) % NX) * NX + (x + dx) % NX
            remote(att_send.at[cc], att_recv.at[i], s3.at[i], r3.at[i], cc, h, p).start()
            return carry

        lax.fori_loop(1 if dy == 0 else 0, NX, send_att, 0)

    def merge(state, block):
        acc, m, l = state
        m_in, l_in = read_stats(block[HD:MSG])
        m_all = jnp.maximum(m, m_in)
        a = jnp.exp(m - m_all)
        b = jnp.exp(m_in - m_all)
        return (acc * a + block[0:HD].astype(F32) * b, m_all, l * a + l_in * b)

    def sum_att(i, state):
        remote(att_send.at[c], att_recv.at[i], s3.at[i], r3.at[i], c, h, p).wait_recv()
        return merge(state, att_recv[i])

    state = lax.fori_loop(1, PLANE, sum_att, (acc_v[c], m_v[c][0:1], l_v[c][0:1]))
    attz_send[0:HD] = state[0].astype(BF16)
    attz_send[HD:MSG] = stat_rows(state[1], state[2])
    swap_att = remote(attz_send, attz_recv, s4, r4, c, h, 1 - p)
    swap_att.start()
    swap_att.wait_recv()
    acc, _, l = merge(state, attz_recv[...])
    att = (acc / l).astype(BF16)
    to = lax.broadcasted_iota(jnp.int32, (CHUNK, CHUNK), 0)
    frm = lax.broadcasted_iota(jnp.int32, (CHUNK, CHUNK), 1)
    perm = jnp.where(frm == (to % 16) * GROUP + to // 16, 1.0, 0.0).astype(BF16)
    ag_v[c] = mm(perm, att, 1, 1).astype(BF16)

    def send_ag(i, carry):
        remote(ag_v.at[c], ag_v.at[c], s5.at[i], r5.at[i], plane_peer(i), h, p).start()
        return carry

    lax.fori_loop(1, PLANE, send_ag, 0)
    loads[9].wait()

    def wait_ag(i, carry):
        src = ((y + NX - i // NX) % NX) * NX + (x + NX - i % NX) % NX
        remote(ag_v.at[c], ag_v.at[src], s5.at[i], r5.at[i], c, h, p).wait_recv()
        return carry

    lax.fori_loop(1, PLANE, wait_ag, 0)

    out = jnp.zeros((256, OUT_COLS), F32)
    for g in range(GROUP):
        a = ag_v[:, g * 16:(g + 1) * 16, :].reshape(256, HD)
        out = out + jnp.dot(a, ow_v[g * HD:(g + 1) * HD, :], preferred_element_type=F32)
    part_v[...] = out.reshape(HEADS, 32, OUT_COLS)
    out_send[...] = out.astype(BF16).reshape(HEADS, 32, OUT_COLS)

    def send_out(j, carry):
        hh = (h + j) % HEADS
        remote(out_send.at[hh], out_recv.at[j], s6.at[j], r6.at[j], c, hh, p).start()
        return carry

    lax.fori_loop(1, HEADS, send_out, 0)

    def sum_out(j, acc):
        remote(out_send.at[h], out_recv.at[j], s6.at[j], r6.at[j], c, h, p).wait_recv()
        return acc + out_recv[j].astype(F32)

    proj_ref[...] = lax.fori_loop(1, HEADS, sum_out, part_v[h]).astype(BF16)

    def drain(i, carry):
        remote(kv_send.at[c], kv_recv.at[i], s1.at[i], r1.at[i], c, h, p).wait_send()
        remote(att_send.at[c], att_recv.at[i], s3.at[i], r3.at[i], c, h, p).wait_send()
        remote(ag_v.at[c], ag_v.at[c], s5.at[i], r5.at[i], c, h, p).wait_send()
        return carry

    lax.fori_loop(1, PLANE, drain, 0)
    swap.wait_send()
    swap_att.wait_send()

    def drain_out(j, carry):
        remote(out_send.at[h], out_recv.at[j], s6.at[j], r6.at[j], c, h, p).wait_send()
        return carry

    lax.fori_loop(1, HEADS, drain_out, 0)


def body(
    queries, prefix_keys, prefix_values, new_states, key_weight, value_weight,
    suffix_keys, suffix_values, suffix_lengths, assignment, out_weight,
):
    rot = jnp.asarray(rotary_tables())
    hbm = pl.BlockSpec(memory_space=pl.ANY)
    vmem = pl.BlockSpec(memory_space=pltpu.VMEM)
    dma = pltpu.SemaphoreType.DMA
    projected, new_keys, new_values = pl.pallas_call(
        kernel,
        out_shape=(
            jax.ShapeDtypeStruct((32, OUT_COLS), BF16),
            jax.ShapeDtypeStruct((NEW_DEV, HD), BF16),
            jax.ShapeDtypeStruct((NEW_DEV, HD), BF16),
        ),
        in_specs=[hbm] * 12,
        out_specs=(vmem, vmem, vmem),
        scratch_shapes=[
            pltpu.VMEM((NEW, FEAT), BF16),
            pltpu.VMEM((FEAT, 2 * HD), BF16),
            pltpu.VMEM((ROWS, HD), BF16),
            pltpu.VMEM((CACHED + SUFFIX, HD), BF16),
            pltpu.VMEM((CACHED + SUFFIX, HD), BF16),
            pltpu.VMEM((HD, CACHED + SUFFIX), BF16),
            pltpu.VMEM((GROUP * HD, OUT_COLS), BF16),
            pltpu.VMEM((NEW_DEV, 2 * HD), F32),
            pltpu.SMEM((1,), jnp.int32),
            pltpu.VMEM((1, 256), jnp.int32),
            pltpu.VMEM((PLANE, NEW_CHIP, 2 * HD), BF16),
            pltpu.VMEM((PLANE, NEW_CHIP, 2 * HD), BF16),
            pltpu.VMEM((NEW_DEV, 2 * HD), BF16),
            pltpu.VMEM((NEW_DEV, 2 * HD), BF16),
            pltpu.VMEM((PLANE, HD, CHUNK), F32),
            pltpu.VMEM((PLANE, 8, CHUNK), F32),
            pltpu.VMEM((PLANE, 8, CHUNK), F32),
            pltpu.VMEM((PLANE, MSG, CHUNK), BF16),
            pltpu.VMEM((PLANE, MSG, CHUNK), BF16),
            pltpu.VMEM((MSG, CHUNK), BF16),
            pltpu.VMEM((MSG, CHUNK), BF16),
            pltpu.VMEM((PLANE, CHUNK, HD), BF16),
            pltpu.VMEM((HEADS, 32, OUT_COLS), F32),
            pltpu.VMEM((HEADS, 32, OUT_COLS), BF16),
            pltpu.VMEM((HEADS, 32, OUT_COLS), BF16),
            dma((12,)),
            dma((PLANE,)), dma((PLANE,)),
            dma, dma,
            dma((PLANE,)), dma((PLANE,)),
            dma, dma,
            dma((PLANE,)), dma((PLANE,)),
            dma((HEADS,)), dma((HEADS,)),
        ],
        compiler_params=pltpu.CompilerParams(
            collective_id=0, has_side_effects=True, vmem_limit_bytes=60 * 1024 * 1024
        ),
    )(
        queries.reshape(ROWS, HD),
        prefix_keys.reshape(CACHED, HD),
        prefix_values.reshape(CACHED, HD),
        new_states,
        key_weight,
        value_weight,
        suffix_keys.reshape(SUFFIX, HD),
        suffix_values.reshape(SUFFIX, HD),
        suffix_lengths,
        assignment.reshape(1, 256),
        out_weight,
        rot,
    )
    return (
        projected,
        new_keys.reshape(NEW_DEV, 1, HD),
        new_values.reshape(NEW_DEV, 1, HD),
    )


def solution(mesh):
    in_specs = (
        P(None, "head", None),
        P(("ctx", "pool"), "head", None),
        P(("ctx", "pool"), "head", None),
        P(None, ("ctx", "pool")),
        P(("ctx", "pool"), "head"),
        P(("ctx", "pool"), "head"),
        P(("ctx", "pool"), None, "head", None),
        P(("ctx", "pool"), None, "head", None),
        P(("ctx", "pool")),
        P(),
        P("head", ("ctx", "pool")),
    )
    out_specs = (
        P("head", ("ctx", "pool")),
        P(("ctx", "pool"), "head", None),
        P(("ctx", "pool"), "head", None),
    )
    return jax.shard_map(body, mesh=mesh, in_specs=in_specs, out_specs=out_specs, check_vma=False)
```

```python
import functools
import math

import jax
import jax.numpy as jnp
import numpy as np
from jax import lax
from jax.experimental import pallas as pl
from jax.experimental.pallas import tpu as pltpu
from jax.sharding import PartitionSpec as P

F32 = jnp.float32
BF16 = jnp.bfloat16
NX = 4
PLANE = 16
POOL = 2
HEADS = 8
GROUP = 8
HD = 128
PREFIX = 8192
NEW = 1536
NEW_DEV = NEW // (PLANE * POOL)
NEW_CHIP = NEW_DEV * POOL
FEAT = 256
ROWS = 2048
CHUNK = 128
CACHED = 256
SUFFIX = 256
MSG = HD + 16
OUT_COLS = 256
SCALE = HD**-0.5
EARLY = 2


def rotary_tables():
    half = HD // 2
    frequency = np.exp(
        np.arange(half, dtype=np.float32) * np.float32(-2.0 * math.log(500000.0) / HD)
    ).astype(np.float32)
    positions = (PREFIX + np.arange(NEW)).astype(np.float32)
    angles = (positions[:, None] * frequency[None, :]).astype(np.float32).astype(np.float64)
    cosine = np.cos(angles).astype(np.float32)
    sine = np.sin(angles).astype(np.float32)
    both = np.concatenate([cosine, cosine, -sine, sine], 1)
    return both.reshape(PLANE, NEW_CHIP, 2 * HD)


def mm(a, b, ca, cb):
    return lax.dot_general(a, b, (((ca,), (cb,)), ((), ())), preferred_element_type=F32)


def stat_rows(m, l):
    m1 = m.astype(BF16).astype(F32)
    r = m - m1
    m2 = r.astype(BF16).astype(F32)
    m3 = r - m2
    l1 = l.astype(BF16).astype(F32)
    r = l - l1
    l2 = r.astype(BF16).astype(F32)
    l3 = r - l2
    row = lax.broadcasted_iota(jnp.int32, (16, CHUNK), 0)
    out = jnp.zeros((16, CHUNK), F32)
    for k, part in enumerate((m1, m2, m3, l1, l2, l3)):
        out = jnp.where(row == k, jnp.broadcast_to(part, (16, CHUNK)), out)
    return out.astype(BF16)


def read_stats(tile):
    t = tile.astype(F32)
    m = (t[0:1] + t[1:2]) + t[2:3]
    l = (t[3:4] + t[4:5]) + t[5:6]
    return m, l


def kernel(
    q_hbm, pk_hbm, pv_hbm, st_hbm, kw_hbm, vw_hbm, sk_hbm, sv_hbm, len_hbm, asg_hbm, ow_hbm, rot_hbm,
    proj_ref, nk_ref, nv_ref,
    st_v, w_v, q_v, k_v, v_v, vt_v, ow_v, rot_v, len_v, asg_v,
    key_send, key_recv, val_send, val_recv, keyz_send, keyz_recv, valz_send, valz_recv, valz_kept,
    acc_v, m_v, l_v,
    att_send, att_recv, attz_send, attz_recv,
    ag_v, part_v, out_send, out_recv,
    lsem, s1, r1, s2, r2, s3, r3, s4, r4, s5, r5, s6, r6, s7, r7, s8, r8,
):
    c = lax.axis_index("ctx")
    h = lax.axis_index("head")
    p = lax.axis_index("pool")
    y = c // NX
    x = c % NX

    def plane_peer(i):
        return ((y + i // NX) % NX) * NX + (x + i % NX) % NX

    def remote(src, dst, ss, rs, cc, hh, pp):
        return pltpu.make_async_remote_copy(
            src_ref=src, dst_ref=dst, send_sem=ss, recv_sem=rs,
            device_id={"ctx": cc, "head": hh, "pool": pp},
            device_id_type=pl.DeviceIdType.MESH,
        )

    shard = c * POOL + p
    loads = [
        pltpu.make_async_copy(st_hbm, st_v, lsem.at[0]),
        pltpu.make_async_copy(kw_hbm, w_v.at[:, pl.ds(0, HD)], lsem.at[1]),
        pltpu.make_async_copy(vw_hbm, w_v.at[:, pl.ds(HD, HD)], lsem.at[2]),
        pltpu.make_async_copy(q_hbm, q_v, lsem.at[3]),
        pltpu.make_async_copy(pk_hbm, k_v.at[pl.ds(0, CACHED)], lsem.at[4]),
        pltpu.make_async_copy(sk_hbm, k_v.at[pl.ds(CACHED, SUFFIX)], lsem.at[5]),
        pltpu.make_async_copy(pv_hbm, v_v.at[pl.ds(0, CACHED)], lsem.at[6]),
        pltpu.make_async_copy(sv_hbm, v_v.at[pl.ds(CACHED, SUFFIX)], lsem.at[7]),
        pltpu.make_async_copy(rot_hbm.at[c], rot_v, lsem.at[8]),
        pltpu.make_async_copy(ow_hbm, ow_v, lsem.at[9]),
        pltpu.make_async_copy(len_hbm, len_v, lsem.at[10]),
        pltpu.make_async_copy(asg_hbm, asg_v, lsem.at[11]),
    ]
    for copy in loads:
        copy.start()

    barrier = pltpu.get_barrier_semaphore()

    def greet(i, carry):
        pl.semaphore_signal(
            barrier, inc=1, device_id={"ctx": plane_peer(i), "head": h, "pool": p},
            device_id_type=pl.DeviceIdType.MESH,
        )
        return carry

    lax.fori_loop(1, PLANE, greet, 0)
    pl.semaphore_signal(
        barrier, inc=1, device_id={"ctx": c, "head": h, "pool": 1 - p},
        device_id_type=pl.DeviceIdType.MESH,
    )

    def greet_head(j, carry):
        pl.semaphore_signal(
            barrier, inc=1, device_id={"ctx": c, "head": (h + j) % HEADS, "pool": p},
            device_id_type=pl.DeviceIdType.MESH,
        )
        return carry

    lax.fori_loop(1, HEADS, greet_head, 0)

    for copy in loads[:3]:
        copy.wait()
    pl.semaphore_wait(barrier, (PLANE - 1) + 1 + (HEADS - 1))

    for dy in (2, 1, 3, 0):
        yy = (y + dy) % NX
        first = pl.multiple_of(yy * (NX * NEW_CHIP), NX * NEW_CHIP)
        part = jnp.dot(st_v[pl.ds(first, NX * NEW_CHIP), :], w_v[...], preferred_element_type=F32)
        part = part.astype(BF16)
        key_send[pl.ds(yy * NX, NX)] = part[:, :HD].reshape(NX, NEW_CHIP, HD)
        val_send[pl.ds(yy * NX, NX)] = part[:, HD:].reshape(NX, NEW_CHIP, HD)

        def send_keys(dx, carry, dy=dy, yy=yy):
            i = dy * NX + dx
            cc = yy * NX + (x + dx) % NX
            remote(key_send.at[cc], key_recv.at[i], s1.at[i], r1.at[i], cc, h, p).start()
            return carry

        lax.fori_loop(1 if dy == 0 else 0, NX, send_keys, 0)

    def send_values(i, carry):
        cc = plane_peer(i)
        remote(val_send.at[cc], val_recv.at[i], s7.at[i], r7.at[i], cc, h, p).start()
        return carry

    for copy in loads[3:8] + loads[10:]:
        copy.wait()
    vt_v[...] = v_v[...].astype(F32).T.astype(BF16)
    suffix_id = shard
    lim = jnp.where(asg_v[...] == suffix_id, len_v[0], 0).astype(BF16)
    lim = jnp.broadcast_to(lim, (16, 256))

    def cached_block(b, carry):
        who = lax.broadcasted_iota(jnp.int32, (256, 256), 0)
        row = lax.broadcasted_iota(jnp.int32, (256, 256), 1)
        spread = jnp.where(who == b * 32 + row // GROUP, 1.0, 0.0).astype(BF16)
        lim_rows = mm(lim, spread, 1, 0)[0:1]
        qb = q_v[pl.ds(pl.multiple_of(b * 256, 256), 256), :]
        s = mm(k_v[...], qb, 1, 1) * SCALE
        key = lax.broadcasted_iota(jnp.int32, (SUFFIX, 256), 0).astype(F32)
        side = jnp.where(key < lim_rows, s[CACHED:], -jnp.inf)
        m = jnp.maximum(
            jnp.max(s[:CACHED], 0, keepdims=True), jnp.max(side, 0, keepdims=True)
        )
        main_e = jnp.exp(s[:CACHED] - m)
        side_e = jnp.exp(side - m)
        l = jnp.sum(main_e, 0, keepdims=True) + jnp.sum(side_e, 0, keepdims=True)
        e = jnp.concatenate([main_e.astype(BF16), side_e.astype(BF16)], 0)
        o = mm(vt_v[...], e, 1, 0)
        for k in range(2):
            lanes = slice(k * CHUNK, (k + 1) * CHUNK)
            acc_v[b * 2 + k] = o[:, lanes]
            m_v[b * 2 + k] = jnp.broadcast_to(m[:, lanes], (8, CHUNK))
            l_v[b * 2 + k] = jnp.broadcast_to(l[:, lanes], (8, CHUNK))
        return carry

    lax.fori_loop(0, EARLY, cached_block, 0)
    lax.fori_loop(1, PLANE, send_values, 0)
    lax.fori_loop(EARLY, 8, cached_block, 0)

    mine = jnp.dot(
        st_v[pl.ds(pl.multiple_of(c * NEW_CHIP, NEW_CHIP), NEW_CHIP), :], w_v[...],
        preferred_element_type=F32,
    )

    def sum_keys(i, acc):
        remote(key_send.at[c], key_recv.at[i], s1.at[i], r1.at[i], c, h, p).wait_recv()
        return acc + key_recv[i].astype(F32)

    keyz_send[...] = lax.fori_loop(1, PLANE, sum_keys, mine[:, :HD])
    swap = remote(keyz_send, keyz_recv, s2, r2, c, h, 1 - p)
    swap.start()

    def sum_values(i, acc):
        remote(val_send.at[c], val_recv.at[i], s7.at[i], r7.at[i], c, h, p).wait_recv()
        return acc + val_recv[i].astype(F32)

    values = lax.fori_loop(1, PLANE, sum_values, mine[:, HD:])
    first = p == 0
    valz_send[...] = jnp.where(first, values[NEW_DEV:], values[:NEW_DEV]).astype(BF16)
    valz_kept[...] = jnp.where(first, values[:NEW_DEV], values[NEW_DEV:])
    swap_values = remote(valz_send, valz_recv, s8, r8, c, h, 1 - p)
    swap_values.start()
    new_vt = values.T.astype(BF16)
    loads[8].wait()
    swap.wait_recv()
    raw = keyz_send[...] + keyz_recv[...]
    turned = pltpu.roll(raw, HD // 2, 1)
    new_k = (raw * rot_v[:, :HD] + turned * rot_v[:, HD:]).astype(BF16)
    nk_ref[...] = jnp.where(first, new_k[:NEW_DEV], new_k[NEW_DEV:])
    token = lax.broadcasted_iota(jnp.int32, (NEW_CHIP, CHUNK), 0)
    counted = jnp.where((token // NEW_DEV) == p, 1.0, 0.0).astype(F32)

    def new_block(dy):
        yy = (y + dy) % NX
        qb = q_v[pl.ds(pl.multiple_of(yy * 512, 512), 512), :]
        s = mm(new_k, qb, 1, 1) * SCALE
        s_max = jnp.max(s, 0, keepdims=True)
        for k in range(NX):
            lanes = slice(k * CHUNK, (k + 1) * CHUNK)
            cc = yy * NX + k
            m_old = m_v[cc][0:1]
            m_new = jnp.maximum(m_old, s_max[:, lanes])
            shrink = jnp.exp(m_old - m_new)
            e = jnp.exp(s[:, lanes] - m_new)
            l_new = l_v[cc][0:1] * shrink + jnp.sum(e * counted, 0, keepdims=True)
            o = acc_v[cc] * shrink + mm(new_vt, e.astype(BF16), 1, 0)
            att_send[cc, 0:HD] = o.astype(BF16)
            att_send[cc, HD:MSG] = stat_rows(m_new, l_new)
            if dy == 0:
                acc_v[cc] = o
                m_v[cc] = jnp.broadcast_to(m_new, (8, CHUNK))
                l_v[cc] = jnp.broadcast_to(l_new, (8, CHUNK))

    for dy in (2, 1, 3, 0):
        new_block(dy)

        def send_att(dx, carry, dy=dy):
            i = dy * NX + dx
            cc = ((y + dy) % NX) * NX + (x + dx) % NX
            remote(att_send.at[cc], att_recv.at[i], s3.at[i], r3.at[i], cc, h, p).start()
            return carry

        lax.fori_loop(1 if dy == 0 else 0, NX, send_att, 0)

    def merge(state, block):
        acc, m, l = state
        m_in, l_in = read_stats(block[HD:MSG])
        m_all = jnp.maximum(m, m_in)
        a = jnp.exp(m - m_all)
        b = jnp.exp(m_in - m_all)
        return (acc * a + block[0:HD].astype(F32) * b, m_all, l * a + l_in * b)

    def sum_att(i, state):
        remote(att_send.at[c], att_recv.at[i], s3.at[i], r3.at[i], c, h, p).wait_recv()
        return merge(state, att_recv[i])

    state = lax.fori_loop(1, PLANE, sum_att, (acc_v[c], m_v[c][0:1], l_v[c][0:1]))
    attz_send[0:HD] = state[0].astype(BF16)
    attz_send[HD:MSG] = stat_rows(state[1], state[2])
    swap_att = remote(attz_send, attz_recv, s4, r4, c, h, 1 - p)
    swap_att.start()
    swap_att.wait_recv()
    acc, _, l = merge(state, attz_recv[...])
    att = (acc / l).astype(BF16)
    to = lax.broadcasted_iota(jnp.int32, (CHUNK, CHUNK), 0)
    frm = lax.broadcasted_iota(jnp.int32, (CHUNK, CHUNK), 1)
    perm = jnp.where(frm == (to % 16) * GROUP + to // 16, 1.0, 0.0).astype(BF16)
    ag_v[c] = mm(perm, att, 1, 1).astype(BF16)

    def send_ag(i, carry):
        remote(ag_v.at[c], ag_v.at[c], s5.at[i], r5.at[i], plane_peer(i), h, p).start()
        return carry

    lax.fori_loop(1, PLANE, send_ag, 0)
    loads[9].wait()

    def wait_ag(i, carry):
        src = ((y + NX - i // NX) % NX) * NX + (x + NX - i % NX) % NX
        remote(ag_v.at[c], ag_v.at[src], s5.at[i], r5.at[i], c, h, p).wait_recv()
        return carry

    lax.fori_loop(1, PLANE, wait_ag, 0)

    out = jnp.zeros((256, OUT_COLS), F32)
    for g in range(GROUP):
        a = ag_v[:, g * 16:(g + 1) * 16, :].reshape(256, HD)
        out = out + jnp.dot(a, ow_v[g * HD:(g + 1) * HD, :], preferred_element_type=F32)
    part_v[...] = out.reshape(HEADS, 32, OUT_COLS)
    out_send[...] = out.astype(BF16).reshape(HEADS, 32, OUT_COLS)

    def send_out(j, carry):
        hh = (h + j) % HEADS
        remote(out_send.at[hh], out_recv.at[j], s6.at[j], r6.at[j], c, hh, p).start()
        return carry

    lax.fori_loop(1, HEADS, send_out, 0)

    def sum_out(j, acc):
        remote(out_send.at[h], out_recv.at[j], s6.at[j], r6.at[j], c, h, p).wait_recv()
        return acc + out_recv[j].astype(F32)

    swap_values.wait_recv()
    nv_ref[...] = (valz_kept[...] + valz_recv[...].astype(F32)).astype(BF16)

    proj_ref[...] = lax.fori_loop(1, HEADS, sum_out, part_v[h]).astype(BF16)

    def drain(i, carry):
        remote(key_send.at[c], key_recv.at[i], s1.at[i], r1.at[i], c, h, p).wait_send()
        remote(val_send.at[c], val_recv.at[i], s7.at[i], r7.at[i], c, h, p).wait_send()
        remote(att_send.at[c], att_recv.at[i], s3.at[i], r3.at[i], c, h, p).wait_send()
        remote(ag_v.at[c], ag_v.at[c], s5.at[i], r5.at[i], c, h, p).wait_send()
        return carry

    lax.fori_loop(1, PLANE, drain, 0)
    swap.wait_send()
    swap_values.wait_send()
    swap_att.wait_send()

    def drain_out(j, carry):
        remote(out_send.at[h], out_recv.at[j], s6.at[j], r6.at[j], c, h, p).wait_send()
        return carry

    lax.fori_loop(1, HEADS, drain_out, 0)


def body(
    queries, prefix_keys, prefix_values, new_states, key_weight, value_weight,
    suffix_keys, suffix_values, suffix_lengths, assignment, out_weight,
):
    rot = jnp.asarray(rotary_tables())
    hbm = pl.BlockSpec(memory_space=pl.ANY)
    vmem = pl.BlockSpec(memory_space=pltpu.VMEM)
    dma = pltpu.SemaphoreType.DMA
    projected, new_keys, new_values = pl.pallas_call(
        kernel,
        out_shape=(
            jax.ShapeDtypeStruct((32, OUT_COLS), BF16),
            jax.ShapeDtypeStruct((NEW_DEV, HD), BF16),
            jax.ShapeDtypeStruct((NEW_DEV, HD), BF16),
        ),
        in_specs=[hbm] * 12,
        out_specs=(vmem, vmem, vmem),
        scratch_shapes=[
            pltpu.VMEM((NEW, FEAT), BF16),
            pltpu.VMEM((FEAT, 2 * HD), BF16),
            pltpu.VMEM((ROWS, HD), BF16),
            pltpu.VMEM((CACHED + SUFFIX, HD), BF16),
            pltpu.VMEM((CACHED + SUFFIX, HD), BF16),
            pltpu.VMEM((HD, CACHED + SUFFIX), BF16),
            pltpu.VMEM((GROUP * HD, OUT_COLS), BF16),
            pltpu.VMEM((NEW_CHIP, 2 * HD), F32),
            pltpu.SMEM((1,), jnp.int32),
            pltpu.VMEM((1, 256), jnp.int32),
            pltpu.VMEM((PLANE, NEW_CHIP, HD), BF16),
            pltpu.VMEM((PLANE, NEW_CHIP, HD), BF16),
            pltpu.VMEM((PLANE, NEW_CHIP, HD), BF16),
            pltpu.VMEM((PLANE, NEW_CHIP, HD), BF16),
            pltpu.VMEM((NEW_CHIP, HD), F32),
            pltpu.VMEM((NEW_CHIP, HD), F32),
            pltpu.VMEM((NEW_DEV, HD), BF16),
            pltpu.VMEM((NEW_DEV, HD), BF16),
            pltpu.VMEM((NEW_DEV, HD), F32),
            pltpu.VMEM((PLANE, HD, CHUNK), F32),
            pltpu.VMEM((PLANE, 8, CHUNK), F32),
            pltpu.VMEM((PLANE, 8, CHUNK), F32),
            pltpu.VMEM((PLANE, MSG, CHUNK), BF16),
            pltpu.VMEM((PLANE, MSG, CHUNK), BF16),
            pltpu.VMEM((MSG, CHUNK), BF16),
            pltpu.VMEM((MSG, CHUNK), BF16),
            pltpu.VMEM((PLANE, CHUNK, HD), BF16),
            pltpu.VMEM((HEADS, 32, OUT_COLS), F32),
            pltpu.VMEM((HEADS, 32, OUT_COLS), BF16),
            pltpu.VMEM((HEADS, 32, OUT_COLS), BF16),
            dma((12,)),
            dma((PLANE,)), dma((PLANE,)),
            dma, dma,
            dma((PLANE,)), dma((PLANE,)),
            dma, dma,
            dma((PLANE,)), dma((PLANE,)),
            dma((HEADS,)), dma((HEADS,)),
            dma((PLANE,)), dma((PLANE,)),
            dma, dma,
        ],
        compiler_params=pltpu.CompilerParams(
            collective_id=0, has_side_effects=True, vmem_limit_bytes=55168 * 1024
        ),
    )(
        queries.reshape(ROWS, HD),
        prefix_keys.reshape(CACHED, HD),
        prefix_values.reshape(CACHED, HD),
        new_states,
        key_weight,
        value_weight,
        suffix_keys.reshape(SUFFIX, HD),
        suffix_values.reshape(SUFFIX, HD),
        suffix_lengths,
        assignment.reshape(1, 256),
        out_weight,
        rot,
    )
    return (
        projected,
        new_keys.reshape(NEW_DEV, 1, HD),
        new_values.reshape(NEW_DEV, 1, HD),
    )


def solution(mesh):
    in_specs = (
        P(None, "head", None),
        P(("ctx", "pool"), "head", None),
        P(("ctx", "pool"), "head", None),
        P(None, ("ctx", "pool")),
        P(("ctx", "pool"), "head"),
        P(("ctx", "pool"), "head"),
        P(("ctx", "pool"), None, "head", None),
        P(("ctx", "pool"), None, "head", None),
        P(("ctx", "pool")),
        P(),
        P("head", ("ctx", "pool")),
    )
    out_specs = (
        P("head", ("ctx", "pool")),
        P(("ctx", "pool"), "head", None),
        P(("ctx", "pool"), "head", None),
    )
    return jax.shard_map(body, mesh=mesh, in_specs=in_specs, out_specs=out_specs, check_vma=False)
```

```python
import functools
import math

import jax
import jax.numpy as jnp
import numpy as np
from jax import lax
from jax.experimental import pallas as pl
from jax.experimental.pallas import tpu as pltpu
from jax.sharding import PartitionSpec as P

F32 = jnp.float32
BF16 = jnp.bfloat16
NX = 4
PLANE = 16
POOL = 2
HEADS = 8
GROUP = 8
HD = 128
PREFIX = 8192
NEW = 1536
NEW_DEV = NEW // (PLANE * POOL)
NEW_CHIP = NEW_DEV * POOL
FEAT = 256
ROWS = 2048
CHUNK = 128
CACHED = 256
SUFFIX = 256
MSG = HD + 16
OUT_COLS = 256
SCALE = HD**-0.5


def hops(i):
    return sum(min(d, NX - d) for d in (i % NX, i // NX))


FARTHEST = sorted(range(1, PLANE), key=lambda i: -hops(i))


def rotary_tables():
    half = HD // 2
    frequency = np.exp(
        np.arange(half, dtype=np.float32) * np.float32(-2.0 * math.log(500000.0) / HD)
    ).astype(np.float32)
    positions = (PREFIX + np.arange(NEW)).astype(np.float32)
    angles = (positions[:, None] * frequency[None, :]).astype(np.float32).astype(np.float64)
    cosine = np.cos(angles).astype(np.float32)
    sine = np.sin(angles).astype(np.float32)
    both = np.concatenate([cosine, cosine, -sine, sine], 1)
    return both.reshape(PLANE, NEW_CHIP, 2 * HD)


def mm(a, b, ca, cb):
    return lax.dot_general(a, b, (((ca,), (cb,)), ((), ())), preferred_element_type=F32)


def stat_rows(m, l):
    m1 = m.astype(BF16).astype(F32)
    r = m - m1
    m2 = r.astype(BF16).astype(F32)
    m3 = r - m2
    l1 = l.astype(BF16).astype(F32)
    r = l - l1
    l2 = r.astype(BF16).astype(F32)
    l3 = r - l2
    row = lax.broadcasted_iota(jnp.int32, (16, CHUNK), 0)
    out = jnp.zeros((16, CHUNK), F32)
    for k, part in enumerate((m1, m2, m3, l1, l2, l3)):
        out = jnp.where(row == k, jnp.broadcast_to(part, (16, CHUNK)), out)
    return out.astype(BF16)


def read_stats(tile):
    t = tile.astype(F32)
    m = (t[0:1] + t[1:2]) + t[2:3]
    l = (t[3:4] + t[4:5]) + t[5:6]
    return m, l


def kernel(
    q_hbm, pk_hbm, pv_hbm, st_hbm, kw_hbm, vw_hbm, sk_hbm, sv_hbm, len_hbm, asg_hbm, ow_hbm, rot_hbm,
    proj_ref, nk_ref, nv_ref,
    st_v, w_v, q_v, k_v, v_v, vt_v, ow_v, rot_v, len_v, asg_v,
    key_send, key_recv, val_send, val_recv, keyz_send, keyz_recv, valz_send, valz_recv, valz_kept,
    acc_v, m_v, l_v,
    att_send, att_recv, attz_send, attz_recv,
    ag_v, part_v, out_send, out_recv,
    lsem, s1, r1, s2, r2, s3, r3, s4, r4, s5, r5, s6, r6, s7, r7, s8, r8,
):
    c = lax.axis_index("ctx")
    h = lax.axis_index("head")
    p = lax.axis_index("pool")
    y = c // NX
    x = c % NX

    def plane_peer(i):
        return ((y + i // NX) % NX) * NX + (x + i % NX) % NX

    def remote(src, dst, ss, rs, cc, hh, pp):
        return pltpu.make_async_remote_copy(
            src_ref=src, dst_ref=dst, send_sem=ss, recv_sem=rs,
            device_id={"ctx": cc, "head": hh, "pool": pp},
            device_id_type=pl.DeviceIdType.MESH,
        )

    barrier = pltpu.get_barrier_semaphore()

    def greet(cc, hh, pp):
        pl.semaphore_signal(
            barrier, inc=1, device_id={"ctx": cc, "head": hh, "pool": pp},
            device_id_type=pl.DeviceIdType.MESH,
        )

    for i in FARTHEST:
        greet(plane_peer(i), h, p)
    greet(c, h, 1 - p)
    for j in range(1, HEADS):
        greet(c, (h + j) % HEADS, p)

    shard = c * POOL + p
    loads = [
        pltpu.make_async_copy(st_hbm, st_v, lsem.at[0]),
        pltpu.make_async_copy(kw_hbm, w_v.at[:, pl.ds(0, HD)], lsem.at[1]),
        pltpu.make_async_copy(vw_hbm, w_v.at[:, pl.ds(HD, HD)], lsem.at[2]),
        pltpu.make_async_copy(q_hbm, q_v, lsem.at[3]),
        pltpu.make_async_copy(pk_hbm, k_v.at[pl.ds(0, CACHED)], lsem.at[4]),
        pltpu.make_async_copy(sk_hbm, k_v.at[pl.ds(CACHED, SUFFIX)], lsem.at[5]),
        pltpu.make_async_copy(pv_hbm, v_v.at[pl.ds(0, CACHED)], lsem.at[6]),
        pltpu.make_async_copy(sv_hbm, v_v.at[pl.ds(CACHED, SUFFIX)], lsem.at[7]),
        pltpu.make_async_copy(rot_hbm.at[c], rot_v, lsem.at[8]),
        pltpu.make_async_copy(ow_hbm, ow_v, lsem.at[9]),
        pltpu.make_async_copy(len_hbm, len_v, lsem.at[10]),
        pltpu.make_async_copy(asg_hbm, asg_v, lsem.at[11]),
    ]
    for copy in loads:
        copy.start()

    for copy in loads[:3]:
        copy.wait()

    for k in range(NX):
        rows = pl.ds(k * NX * NEW_CHIP, NX * NEW_CHIP)
        part = jnp.dot(st_v[rows, :], w_v[...], preferred_element_type=F32).astype(BF16)
        key_send[k * NX:(k + 1) * NX] = part[:, :HD].reshape(NX, NEW_CHIP, HD)
        val_send[k * NX:(k + 1) * NX] = part[:, HD:].reshape(NX, NEW_CHIP, HD)
    pl.semaphore_wait(barrier, (PLANE - 1) + 1 + (HEADS - 1))
    for i in FARTHEST:
        cc = plane_peer(i)
        remote(key_send.at[cc], key_recv.at[i], s1.at[i], r1.at[i], cc, h, p).start()
    for i in FARTHEST:
        cc = plane_peer(i)
        remote(val_send.at[cc], val_recv.at[i], s7.at[i], r7.at[i], cc, h, p).start()

    def drain(src, dst, ss, rs):
        def left(i, carry):
            remote(src.at[c], dst.at[i], ss.at[i], rs.at[i], c, h, p).wait_send()
            return carry

        lax.fori_loop(1, PLANE, left, 0)

    for copy in loads[3:8] + loads[10:]:
        copy.wait()
    vt_v[...] = v_v[...].astype(F32).T.astype(BF16)
    suffix_id = shard
    lim = jnp.where(asg_v[...] == suffix_id, len_v[0], 0).astype(BF16)
    lim = jnp.broadcast_to(lim, (16, 256))

    def cached_block(b, carry):
        who = lax.broadcasted_iota(jnp.int32, (256, 256), 0)
        row = lax.broadcasted_iota(jnp.int32, (256, 256), 1)
        spread = jnp.where(who == b * 32 + row // GROUP, 1.0, 0.0).astype(BF16)
        lim_rows = mm(lim, spread, 1, 0)[0:1]
        qb = q_v[pl.ds(pl.multiple_of(b * 256, 256), 256), :]
        s = mm(k_v[...], qb, 1, 1) * SCALE
        key = lax.broadcasted_iota(jnp.int32, (SUFFIX, 256), 0).astype(F32)
        side = jnp.where(key < lim_rows, s[CACHED:], -jnp.inf)
        m = jnp.maximum(
            jnp.max(s[:CACHED], 0, keepdims=True), jnp.max(side, 0, keepdims=True)
        )
        main_e = jnp.exp(s[:CACHED] - m)
        side_e = jnp.exp(side - m)
        l = jnp.sum(main_e, 0, keepdims=True) + jnp.sum(side_e, 0, keepdims=True)
        e = jnp.concatenate([main_e.astype(BF16), side_e.astype(BF16)], 0)
        o = mm(vt_v[...], e, 1, 0)
        for k in range(2):
            lanes = slice(k * CHUNK, (k + 1) * CHUNK)
            acc_v[b * 2 + k] = o[:, lanes]
            m_v[b * 2 + k] = jnp.broadcast_to(m[:, lanes], (8, CHUNK))
            l_v[b * 2 + k] = jnp.broadcast_to(l[:, lanes], (8, CHUNK))
        return carry

    lax.fori_loop(0, 8, cached_block, 0)

    mine = jnp.dot(
        st_v[pl.ds(pl.multiple_of(c * NEW_CHIP, NEW_CHIP), NEW_CHIP), :], w_v[...],
        preferred_element_type=F32,
    )

    def sum_keys(i, acc):
        remote(key_send.at[c], key_recv.at[i], s1.at[i], r1.at[i], c, h, p).wait_recv()
        return acc + key_recv[i].astype(F32)

    keyz_send[...] = lax.fori_loop(1, PLANE, sum_keys, mine[:, :HD])
    swap = remote(keyz_send, keyz_recv, s2, r2, c, h, 1 - p)
    swap.start()
    drain(key_send, key_recv, s1, r1)

    def sum_values(i, acc):
        remote(val_send.at[c], val_recv.at[i], s7.at[i], r7.at[i], c, h, p).wait_recv()
        return acc + val_recv[i].astype(F32)

    values = lax.fori_loop(1, PLANE, sum_values, mine[:, HD:])
    first = p == 0
    valz_send[...] = jnp.where(first, values[NEW_DEV:], values[:NEW_DEV]).astype(BF16)
    valz_kept[...] = jnp.where(first, values[:NEW_DEV], values[NEW_DEV:])
    swap_values = remote(valz_send, valz_recv, s8, r8, c, h, 1 - p)
    swap_values.start()
    new_vt = values.T.astype(BF16)
    loads[8].wait()
    swap.wait_recv()
    raw = keyz_send[...] + keyz_recv[...]
    turned = pltpu.roll(raw, HD // 2, 1)
    new_k = (raw * rot_v[:, :HD] + turned * rot_v[:, HD:]).astype(BF16)
    nk_ref[...] = jnp.where(first, new_k[:NEW_DEV], new_k[NEW_DEV:])
    token = lax.broadcasted_iota(jnp.int32, (NEW_CHIP, CHUNK), 0)
    counted = jnp.where((token // NEW_DEV) == p, 1.0, 0.0).astype(F32)

    def new_block(dy):
        yy = (y + dy) % NX
        qb = q_v[pl.ds(pl.multiple_of(yy * 512, 512), 512), :]
        s = mm(new_k, qb, 1, 1) * SCALE
        s_max = jnp.max(s, 0, keepdims=True)
        for k in range(NX):
            lanes = slice(k * CHUNK, (k + 1) * CHUNK)
            cc = yy * NX + k
            m_old = m_v[cc][0:1]
            m_new = jnp.maximum(m_old, s_max[:, lanes])
            shrink = jnp.exp(m_old - m_new)
            e = jnp.exp(s[:, lanes] - m_new)
            l_new = l_v[cc][0:1] * shrink + jnp.sum(e * counted, 0, keepdims=True)
            o = acc_v[cc] * shrink + mm(new_vt, e.astype(BF16), 1, 0)
            att_send[cc, 0:HD] = o.astype(BF16)
            att_send[cc, HD:MSG] = stat_rows(m_new, l_new)
            if dy == 0:
                acc_v[cc] = o
                m_v[cc] = jnp.broadcast_to(m_new, (8, CHUNK))
                l_v[cc] = jnp.broadcast_to(l_new, (8, CHUNK))

    for dy in (2, 1, 3, 0):
        new_block(dy)

        for dx in (2, 1, 3, 0):
            i = dy * NX + dx
            if i > 0:
                cc = plane_peer(i)
                remote(att_send.at[cc], att_recv.at[i], s3.at[i], r3.at[i], cc, h, p).start()

    drain(val_send, val_recv, s7, r7)
    swap.wait_send()

    def merge(state, block):
        acc, m, l = state
        m_in, l_in = read_stats(block[HD:MSG])
        m_all = jnp.maximum(m, m_in)
        a = jnp.exp(m - m_all)
        b = jnp.exp(m_in - m_all)
        return (acc * a + block[0:HD].astype(F32) * b, m_all, l * a + l_in * b)

    def sum_att(i, state):
        remote(att_send.at[c], att_recv.at[i], s3.at[i], r3.at[i], c, h, p).wait_recv()
        return merge(state, att_recv[i])

    state = lax.fori_loop(1, PLANE, sum_att, (acc_v[c], m_v[c][0:1], l_v[c][0:1]))
    attz_send[0:HD] = state[0].astype(BF16)
    attz_send[HD:MSG] = stat_rows(state[1], state[2])
    swap_att = remote(attz_send, attz_recv, s4, r4, c, h, 1 - p)
    swap_att.start()
    to = lax.broadcasted_iota(jnp.int32, (CHUNK, CHUNK), 0)
    frm = lax.broadcasted_iota(jnp.int32, (CHUNK, CHUNK), 1)
    perm = jnp.where(frm == (to % 16) * GROUP + to // 16, 1.0, 0.0).astype(BF16)
    drain(att_send, att_recv, s3, r3)
    swap_att.wait_recv()
    acc, _, l = merge(state, attz_recv[...])
    att = (acc / l).astype(BF16)
    ag_v[c] = mm(perm, att, 1, 1).astype(BF16)

    for i in FARTHEST:
        remote(ag_v.at[c], ag_v.at[c], s5.at[i], r5.at[i], plane_peer(i), h, p).start()
    swap_values.wait_recv()
    nv_ref[...] = (valz_kept[...] + valz_recv[...].astype(F32)).astype(BF16)
    swap_values.wait_send()
    swap_att.wait_send()
    loads[9].wait()

    for dy in (0, 1, 3, 2):
        yy = (y + NX - dy) % NX
        for dx in range(NX):
            i = dy * NX + dx
            if i > 0:
                src = yy * NX + (x + NX - dx) % NX
                remote(ag_v.at[c], ag_v.at[src], s5.at[i], r5.at[i], c, h, p).wait_recv()
        rows = ag_v[pl.ds(yy * NX, NX)]
        out = jnp.zeros((NX * 16, OUT_COLS), F32)
        for g in range(0, GROUP, 2):
            a = jnp.concatenate(
                [rows[:, (g + k) * 16:(g + k + 1) * 16, :].reshape(NX * 16, HD) for k in range(2)], 1
            )
            out = out + jnp.dot(a, ow_v[g * HD:(g + 2) * HD, :], preferred_element_type=F32)
        part_v[pl.ds(yy * 2, 2)] = out.reshape(2, 32, OUT_COLS)
        out_send[pl.ds(yy * 2, 2)] = out.astype(BF16).reshape(2, 32, OUT_COLS)
        for k in range(2):
            hh = yy * 2 + k
            j = (hh + HEADS - h) % HEADS

            @pl.when(j != 0)
            def _():
                remote(out_send.at[hh], out_recv.at[j], s6.at[j], r6.at[j], c, hh, p).start()

    def left_ag(i, carry):
        remote(ag_v.at[c], ag_v.at[c], s5.at[i], r5.at[i], c, h, p).wait_send()
        return carry

    lax.fori_loop(1, PLANE, left_ag, 0)

    def sum_out(j, acc):
        remote(out_send.at[h], out_recv.at[j], s6.at[j], r6.at[j], c, h, p).wait_recv()
        return acc + out_recv[j].astype(F32)

    proj_ref[...] = lax.fori_loop(1, HEADS, sum_out, part_v[h]).astype(BF16)

    def left_out(j, carry):
        remote(out_send.at[h], out_recv.at[j], s6.at[j], r6.at[j], c, h, p).wait_send()
        return carry

    lax.fori_loop(1, HEADS, left_out, 0)


def body(
    queries, prefix_keys, prefix_values, new_states, key_weight, value_weight,
    suffix_keys, suffix_values, suffix_lengths, assignment, out_weight,
):
    rot = jnp.asarray(rotary_tables())
    hbm = pl.BlockSpec(memory_space=pl.ANY)
    vmem = pl.BlockSpec(memory_space=pltpu.VMEM)
    dma = pltpu.SemaphoreType.DMA
    projected, new_keys, new_values = pl.pallas_call(
        kernel,
        out_shape=(
            jax.ShapeDtypeStruct((32, OUT_COLS), BF16),
            jax.ShapeDtypeStruct((NEW_DEV, HD), BF16),
            jax.ShapeDtypeStruct((NEW_DEV, HD), BF16),
        ),
        in_specs=[hbm] * 12,
        out_specs=(vmem, vmem, vmem),
        scratch_shapes=[
            pltpu.VMEM((NEW, FEAT), BF16),
            pltpu.VMEM((FEAT, 2 * HD), BF16),
            pltpu.VMEM((ROWS, HD), BF16),
            pltpu.VMEM((CACHED + SUFFIX, HD), BF16),
            pltpu.VMEM((CACHED + SUFFIX, HD), BF16),
            pltpu.VMEM((HD, CACHED + SUFFIX), BF16),
            pltpu.VMEM((GROUP * HD, OUT_COLS), BF16),
            pltpu.VMEM((NEW_CHIP, 2 * HD), F32),
            pltpu.SMEM((1,), jnp.int32),
            pltpu.VMEM((1, 256), jnp.int32),
            pltpu.VMEM((PLANE, NEW_CHIP, HD), BF16),
            pltpu.VMEM((PLANE, NEW_CHIP, HD), BF16),
            pltpu.VMEM((PLANE, NEW_CHIP, HD), BF16),
            pltpu.VMEM((PLANE, NEW_CHIP, HD), BF16),
            pltpu.VMEM((NEW_CHIP, HD), F32),
            pltpu.VMEM((NEW_CHIP, HD), F32),
            pltpu.VMEM((NEW_DEV, HD), BF16),
            pltpu.VMEM((NEW_DEV, HD), BF16),
            pltpu.VMEM((NEW_DEV, HD), F32),
            pltpu.VMEM((PLANE, HD, CHUNK), F32),
            pltpu.VMEM((PLANE, 8, CHUNK), F32),
            pltpu.VMEM((PLANE, 8, CHUNK), F32),
            pltpu.VMEM((PLANE, MSG, CHUNK), BF16),
            pltpu.VMEM((PLANE, MSG, CHUNK), BF16),
            pltpu.VMEM((MSG, CHUNK), BF16),
            pltpu.VMEM((MSG, CHUNK), BF16),
            pltpu.VMEM((PLANE, CHUNK, HD), BF16),
            pltpu.VMEM((HEADS, 32, OUT_COLS), F32),
            pltpu.VMEM((HEADS, 32, OUT_COLS), BF16),
            pltpu.VMEM((HEADS, 32, OUT_COLS), BF16),
            dma((12,)),
            dma((PLANE,)), dma((PLANE,)),
            dma, dma,
            dma((PLANE,)), dma((PLANE,)),
            dma, dma,
            dma((PLANE,)), dma((PLANE,)),
            dma((HEADS,)), dma((HEADS,)),
            dma((PLANE,)), dma((PLANE,)),
            dma, dma,
        ],
        compiler_params=pltpu.CompilerParams(
            collective_id=0, has_side_effects=True, vmem_limit_bytes=55168 * 1024
        ),
    )(
        queries.reshape(ROWS, HD),
        prefix_keys.reshape(CACHED, HD),
        prefix_values.reshape(CACHED, HD),
        new_states,
        key_weight,
        value_weight,
        suffix_keys.reshape(SUFFIX, HD),
        suffix_values.reshape(SUFFIX, HD),
        suffix_lengths,
        assignment.reshape(1, 256),
        out_weight,
        rot,
    )
    return (
        projected,
        new_keys.reshape(NEW_DEV, 1, HD),
        new_values.reshape(NEW_DEV, 1, HD),
    )


def solution(mesh):
    in_specs = (
        P(None, "head", None),
        P(("ctx", "pool"), "head", None),
        P(("ctx", "pool"), "head", None),
        P(None, ("ctx", "pool")),
        P(("ctx", "pool"), "head"),
        P(("ctx", "pool"), "head"),
        P(("ctx", "pool"), None, "head", None),
        P(("ctx", "pool"), None, "head", None),
        P(("ctx", "pool")),
        P(),
        P("head", ("ctx", "pool")),
    )
    out_specs = (
        P("head", ("ctx", "pool")),
        P(("ctx", "pool"), "head", None),
        P(("ctx", "pool"), "head", None),
    )
    return jax.shard_map(body, mesh=mesh, in_specs=in_specs, out_specs=out_specs, check_vma=False)
```

```python
import functools
import math

import jax
import jax.numpy as jnp
import numpy as np
from jax import lax
from jax.experimental import pallas as pl
from jax.experimental.pallas import tpu as pltpu
from jax.sharding import PartitionSpec as P

F32 = jnp.float32
BF16 = jnp.bfloat16
NX = 4
PLANE = 16
POOL = 2
HEADS = 8
GROUP = 8
HD = 128
PREFIX = 8192
NEW = 1536
NEW_DEV = NEW // (PLANE * POOL)
NEW_CHIP = NEW_DEV * POOL
FEAT = 256
ROWS = 2048
CHUNK = 128
CACHED = 256
SUFFIX = 256
HALF = HD // 2
FIRST = HALF + 16
OUT_COLS = 256
SCALE = HD**-0.5


def hops(i):
    return sum(min(d, NX - d) for d in (i % NX, i // NX))


FARTHEST = sorted(range(1, PLANE), key=lambda i: -hops(i))


def rotary_tables():
    half = HD // 2
    frequency = np.exp(
        np.arange(half, dtype=np.float32) * np.float32(-2.0 * math.log(500000.0) / HD)
    ).astype(np.float32)
    positions = (PREFIX + np.arange(NEW)).astype(np.float32)
    angles = (positions[:, None] * frequency[None, :]).astype(np.float32).astype(np.float64)
    cosine = np.cos(angles).astype(np.float32)
    sine = np.sin(angles).astype(np.float32)
    both = np.concatenate([cosine, cosine, -sine, sine], 1)
    return both.reshape(PLANE, NEW_CHIP, 2 * HD)


def mm(a, b, ca, cb):
    return lax.dot_general(a, b, (((ca,), (cb,)), ((), ())), preferred_element_type=F32)


def stat_rows(m, l):
    m1 = m.astype(BF16).astype(F32)
    r = m - m1
    m2 = r.astype(BF16).astype(F32)
    m3 = r - m2
    l1 = l.astype(BF16).astype(F32)
    r = l - l1
    l2 = r.astype(BF16).astype(F32)
    l3 = r - l2
    row = lax.broadcasted_iota(jnp.int32, (16, CHUNK), 0)
    out = jnp.zeros((16, CHUNK), F32)
    for k, part in enumerate((m1, m2, m3, l1, l2, l3)):
        out = jnp.where(row == k, jnp.broadcast_to(part, (16, CHUNK)), out)
    return out.astype(BF16)


def read_stats(tile):
    t = tile.astype(F32)
    m = (t[0:1] + t[1:2]) + t[2:3]
    l = (t[3:4] + t[4:5]) + t[5:6]
    return m, l


def kernel(
    q_hbm, pk_hbm, pv_hbm, st_hbm, kw_hbm, vw_hbm, sk_hbm, sv_hbm, len_hbm, asg_hbm, ow_hbm, rot_hbm,
    proj_ref, kv_ref,
    st_v, w_v, q_v, k_v, v_v, vt_v, ow_v, rot_v, len_v, asg_v,
    key_send, key_recv, val_send, val_recv, keyz_send, keyz_recv, valz_send, valz_recv, valz_kept,
    acc_v, m_v, l_v,
    low_send, low_recv, high_send, high_recv, lowz_send, lowz_recv, highz_send, highz_recv,
    ag_v, part_v, out_send, out_recv,
    lsem, wsem, s1, r1, s2, r2, s3, r3, s4, r4, s5, r5, s6, r6, s7, r7, s8, r8, s9, r9, s10, r10, s11, r11,
):
    c = lax.axis_index("ctx")
    h = lax.axis_index("head")
    p = lax.axis_index("pool")
    y = c // NX
    x = c % NX

    def plane_peer(i):
        return ((y + i // NX) % NX) * NX + (x + i % NX) % NX

    def remote(src, dst, ss, rs, cc, hh, pp):
        return pltpu.make_async_remote_copy(
            src_ref=src, dst_ref=dst, send_sem=ss, recv_sem=rs,
            device_id={"ctx": cc, "head": hh, "pool": pp},
            device_id_type=pl.DeviceIdType.MESH,
        )

    barrier = pltpu.get_barrier_semaphore()

    def greet(cc, hh, pp):
        pl.semaphore_signal(
            barrier, inc=1, device_id={"ctx": cc, "head": hh, "pool": pp},
            device_id_type=pl.DeviceIdType.MESH,
        )

    for i in FARTHEST:
        greet(plane_peer(i), h, p)
    greet(c, h, 1 - p)
    for j in range(1, HEADS):
        greet(c, (h + j) % HEADS, p)

    shard = c * POOL + p
    loads = [
        pltpu.make_async_copy(st_hbm, st_v, lsem.at[0]),
        pltpu.make_async_copy(kw_hbm, w_v.at[:, pl.ds(0, HD)], lsem.at[1]),
        pltpu.make_async_copy(vw_hbm, w_v.at[:, pl.ds(HD, HD)], lsem.at[2]),
        pltpu.make_async_copy(q_hbm, q_v, lsem.at[3]),
        pltpu.make_async_copy(pk_hbm, k_v.at[pl.ds(0, CACHED)], lsem.at[4]),
        pltpu.make_async_copy(sk_hbm, k_v.at[pl.ds(CACHED, SUFFIX)], lsem.at[5]),
        pltpu.make_async_copy(pv_hbm, v_v.at[pl.ds(0, CACHED)], lsem.at[6]),
        pltpu.make_async_copy(sv_hbm, v_v.at[pl.ds(CACHED, SUFFIX)], lsem.at[7]),
        pltpu.make_async_copy(rot_hbm.at[c], rot_v, lsem.at[8]),
        pltpu.make_async_copy(len_hbm, len_v, lsem.at[9]),
        pltpu.make_async_copy(asg_hbm, asg_v, lsem.at[10]),
    ]
    weights = [
        pltpu.make_async_copy(
            ow_hbm.at[pl.ds(g * HD + f * HALF, HALF)],
            ow_v.at[f, pl.ds(g * HALF, HALF)],
            wsem.at[f * GROUP + g],
        )
        for f in range(2)
        for g in range(GROUP)
    ]
    for copy in loads + weights:
        copy.start()

    for copy in loads[:3]:
        copy.wait()

    for k in range(NX):
        rows = pl.ds(k * NX * NEW_CHIP, NX * NEW_CHIP)
        part = jnp.dot(st_v[rows, :], w_v[...], preferred_element_type=F32).astype(BF16)
        key_send[k * NX:(k + 1) * NX] = part[:, :HD].reshape(NX, NEW_CHIP, HD)
        val_send[k * NX:(k + 1) * NX] = part[:, HD:].reshape(NX, NEW_CHIP, HD)
    pl.semaphore_wait(barrier, (PLANE - 1) + 1 + (HEADS - 1))
    for i in FARTHEST:
        cc = plane_peer(i)
        remote(key_send.at[cc], key_recv.at[i], s1.at[i], r1.at[i], cc, h, p).start()
    for i in FARTHEST:
        cc = plane_peer(i)
        remote(val_send.at[cc], val_recv.at[i], s7.at[i], r7.at[i], cc, h, p).start()

    def drain(src, dst, ss, rs):
        def left(i, carry):
            remote(src.at[c], dst.at[i], ss.at[i], rs.at[i], c, h, p).wait_send()
            return carry

        lax.fori_loop(1, PLANE, left, 0)

    for copy in loads[3:8] + loads[9:]:
        copy.wait()
    vt_v[...] = v_v[...].astype(F32).T.astype(BF16)
    suffix_id = shard
    lim = jnp.where(asg_v[...] == suffix_id, len_v[0], 0).astype(BF16)
    lim = jnp.broadcast_to(lim, (16, 256))

    def cached_block(b, carry):
        who = lax.broadcasted_iota(jnp.int32, (256, 256), 0)
        row = lax.broadcasted_iota(jnp.int32, (256, 256), 1)
        spread = jnp.where(who == b * 32 + row // GROUP, 1.0, 0.0).astype(BF16)
        lim_rows = mm(lim, spread, 1, 0)[0:1]
        qb = q_v[pl.ds(pl.multiple_of(b * 256, 256), 256), :]
        s = mm(k_v[...], qb, 1, 1) * SCALE
        key = lax.broadcasted_iota(jnp.int32, (SUFFIX, 256), 0).astype(F32)
        side = jnp.where(key < lim_rows, s[CACHED:], -jnp.inf)
        m = jnp.maximum(
            jnp.max(s[:CACHED], 0, keepdims=True), jnp.max(side, 0, keepdims=True)
        )
        main_e = jnp.exp(s[:CACHED] - m)
        side_e = jnp.exp(side - m)
        l = jnp.sum(main_e, 0, keepdims=True) + jnp.sum(side_e, 0, keepdims=True)
        e = jnp.concatenate([main_e.astype(BF16), side_e.astype(BF16)], 0)
        o = mm(vt_v[...], e, 1, 0)
        for k in range(2):
            lanes = slice(k * CHUNK, (k + 1) * CHUNK)
            acc_v[b * 2 + k] = o[:, lanes]
            m_v[b * 2 + k] = jnp.broadcast_to(m[:, lanes], (8, CHUNK))
            l_v[b * 2 + k] = jnp.broadcast_to(l[:, lanes], (8, CHUNK))
        return carry

    lax.fori_loop(0, 8, cached_block, 0)

    mine = jnp.dot(
        st_v[pl.ds(pl.multiple_of(c * NEW_CHIP, NEW_CHIP), NEW_CHIP), :], w_v[...],
        preferred_element_type=F32,
    )

    def sum_keys(i, acc):
        remote(key_send.at[c], key_recv.at[i], s1.at[i], r1.at[i], c, h, p).wait_recv()
        return acc + key_recv[i].astype(F32)

    keyz_send[...] = lax.fori_loop(1, PLANE, sum_keys, mine[:, :HD])
    swap = remote(keyz_send, keyz_recv, s2, r2, c, h, 1 - p)
    swap.start()
    drain(key_send, key_recv, s1, r1)

    def sum_values(i, acc):
        remote(val_send.at[c], val_recv.at[i], s7.at[i], r7.at[i], c, h, p).wait_recv()
        return acc + val_recv[i].astype(F32)

    values = lax.fori_loop(1, PLANE, sum_values, mine[:, HD:])
    first = p == 0
    valz_send[...] = jnp.where(first, values[NEW_DEV:], values[:NEW_DEV]).astype(BF16)
    valz_kept[...] = jnp.where(first, values[:NEW_DEV], values[NEW_DEV:])
    swap_values = remote(valz_send, valz_recv, s8, r8, c, h, 1 - p)
    swap_values.start()
    new_vt = values.T.astype(BF16)
    loads[8].wait()
    swap.wait_recv()
    raw = keyz_send[...] + keyz_recv[...]
    turned = pltpu.roll(raw, HD // 2, 1)
    new_k = (raw * rot_v[:, :HD] + turned * rot_v[:, HD:]).astype(BF16)
    kv_ref[0] = jnp.where(first, new_k[:NEW_DEV], new_k[NEW_DEV:])
    token = lax.broadcasted_iota(jnp.int32, (NEW_CHIP, CHUNK), 0)
    counted = jnp.where((token // NEW_DEV) == p, 1.0, 0.0).astype(F32)

    def new_block(dy):
        yy = (y + dy) % NX
        qb = q_v[pl.ds(pl.multiple_of(yy * 512, 512), 512), :]
        s = mm(new_k, qb, 1, 1) * SCALE
        s_max = jnp.max(s, 0, keepdims=True)
        for k in range(NX):
            lanes = slice(k * CHUNK, (k + 1) * CHUNK)
            cc = yy * NX + k
            m_old = m_v[cc][0:1]
            m_new = jnp.maximum(m_old, s_max[:, lanes])
            shrink = jnp.exp(m_old - m_new)
            e = jnp.exp(s[:, lanes] - m_new)
            l_new = l_v[cc][0:1] * shrink + jnp.sum(e * counted, 0, keepdims=True)
            o = acc_v[cc] * shrink + mm(new_vt, e.astype(BF16), 1, 0)
            low_send[cc, 0:HALF] = o[:HALF].astype(BF16)
            low_send[cc, HALF:FIRST] = stat_rows(m_new, l_new)
            high_send[cc] = o[HALF:].astype(BF16)
            if dy == 0:
                acc_v[cc] = o
                m_v[cc] = jnp.broadcast_to(m_new, (8, CHUNK))
                l_v[cc] = jnp.broadcast_to(l_new, (8, CHUNK))

    for dy in (2, 1, 3, 0):
        new_block(dy)

        for dx in (2, 1, 3, 0):
            i = dy * NX + dx
            if i > 0:
                cc = plane_peer(i)
                remote(low_send.at[cc], low_recv.at[i], s3.at[i], r3.at[i], cc, h, p).start()
    for i in FARTHEST:
        cc = plane_peer(i)
        remote(low_send.at[cc], low_recv.at[i], s3.at[i], r3.at[i], cc, h, p).wait_send()
        remote(high_send.at[cc], high_recv.at[i], s9.at[i], r9.at[i], cc, h, p).start()

    drain(val_send, val_recv, s7, r7)
    swap.wait_send()

    def sum_low(i, state):
        remote(low_send.at[c], low_recv.at[i], s3.at[i], r3.at[i], c, h, p).wait_recv()
        acc, m, l = state
        m_in, l_in = read_stats(low_recv[i, HALF:FIRST])
        m_all = jnp.maximum(m, m_in)
        a = jnp.exp(m - m_all)
        b = jnp.exp(m_in - m_all)
        return (acc * a + low_recv[i, 0:HALF].astype(F32) * b, m_all, l * a + l_in * b)

    own_m = m_v[c][0:1]
    low, m, l = lax.fori_loop(1, PLANE, sum_low, (acc_v[c, 0:HALF], own_m, l_v[c][0:1]))
    lowz_send[0:HALF] = low.astype(BF16)
    lowz_send[HALF:FIRST] = stat_rows(m, l)
    swap_low = remote(lowz_send, lowz_recv, s4, r4, c, h, 1 - p)
    swap_low.start()

    def sum_high(i, acc):
        remote(high_send.at[c], high_recv.at[i], s9.at[i], r9.at[i], c, h, p).wait_recv()
        m_in, _ = read_stats(low_recv[i, HALF:FIRST])
        return acc + high_recv[i].astype(F32) * jnp.exp(m_in - m)

    high = lax.fori_loop(1, PLANE, sum_high, acc_v[c, HALF:HD] * jnp.exp(own_m - m))
    highz_send[...] = high.astype(BF16)
    swap_high = remote(highz_send, highz_recv, s10, r10, c, h, 1 - p)
    swap_high.start()

    to = lax.broadcasted_iota(jnp.int32, (HALF, CHUNK), 0)
    frm = lax.broadcasted_iota(jnp.int32, (HALF, CHUNK), 1)
    perms = [
        jnp.where(frm == (to % 16) * GROUP + (to // 16) * 2 + k, 1.0, 0.0).astype(BF16)
        for k in range(2)
    ]
    drain(high_send, high_recv, s9, r9)

    swap_low.wait_recv()
    m_in, l_in = read_stats(lowz_recv[HALF:FIRST])
    m_all = jnp.maximum(m, m_in)
    a = jnp.exp(m - m_all)
    b = jnp.exp(m_in - m_all)
    inverse = 1.0 / (l * a + l_in * b)
    a, b = a * inverse, b * inverse

    def share(f, mine, other, ss, rs):
        att = (mine * a + other.astype(F32) * b).astype(BF16)
        ag_v[f, c] = jnp.concatenate([mm(perm, att, 1, 1) for perm in perms], 1).astype(BF16)
        for i in FARTHEST:
            remote(ag_v.at[f, c], ag_v.at[f, c], ss.at[i], rs.at[i], plane_peer(i), h, p).start()

    share(0, low, lowz_recv[0:HALF], s5, r5)
    swap_high.wait_recv()
    share(1, high, highz_recv[...], s11, r11)
    swap_values.wait_recv()
    kv_ref[1] = (valz_kept[...] + valz_recv[...].astype(F32)).astype(BF16)
    swap_values.wait_send()
    swap_low.wait_send()
    swap_high.wait_send()
    for copy in weights:
        copy.wait()

    def product(f, yy, dy, ss, rs):
        for dx in range(NX):
            i = dy * NX + dx
            if i > 0:
                src = yy * NX + (x + NX - dx) % NX
                remote(ag_v.at[f, c], ag_v.at[f, src], ss.at[i], rs.at[i], c, h, p).wait_recv()
        rows = ag_v[f, pl.ds(yy * NX, NX)]
        rows = jnp.concatenate(
            [rows[:, k * 16:(k + 1) * 16, :].reshape(NX * 16, HD) for k in range(GROUP // 2)], 1
        )
        return jnp.dot(rows, ow_v[f], preferred_element_type=F32)

    for dy in (0, 1, 3, 2):
        yy = (y + NX - dy) % NX
        part_v[pl.ds(yy * 2, 2)] = product(0, yy, dy, s5, r5).reshape(2, 32, OUT_COLS)
    for dy in (0, 1, 3, 2):
        yy = (y + NX - dy) % NX
        out = part_v[pl.ds(yy * 2, 2)].reshape(NX * 16, OUT_COLS) + product(1, yy, dy, s11, r11)
        part_v[pl.ds(yy * 2, 2)] = out.reshape(2, 32, OUT_COLS)
        out_send[pl.ds(yy * 2, 2)] = out.astype(BF16).reshape(2, 32, OUT_COLS)
        for k in range(2):
            hh = yy * 2 + k
            j = (hh + HEADS - h) % HEADS

            @pl.when(j != 0)
            def _():
                remote(out_send.at[hh], out_recv.at[j], s6.at[j], r6.at[j], c, hh, p).start()

    def left_ag(i, carry):
        remote(ag_v.at[0, c], ag_v.at[0, c], s5.at[i], r5.at[i], c, h, p).wait_send()
        remote(ag_v.at[1, c], ag_v.at[1, c], s11.at[i], r11.at[i], c, h, p).wait_send()
        return carry

    lax.fori_loop(1, PLANE, left_ag, 0)

    def sum_out(j, acc):
        remote(out_send.at[h], out_recv.at[j], s6.at[j], r6.at[j], c, h, p).wait_recv()
        return acc + out_recv[j].astype(F32)

    proj_ref[...] = lax.fori_loop(1, HEADS, sum_out, part_v[h]).astype(BF16)

    def left_out(j, carry):
        remote(out_send.at[h], out_recv.at[j], s6.at[j], r6.at[j], c, h, p).wait_send()
        return carry

    lax.fori_loop(1, HEADS, left_out, 0)


def body(
    queries, prefix_keys, prefix_values, new_states, key_weight, value_weight,
    suffix_keys, suffix_values, suffix_lengths, assignment, out_weight,
):
    rot = jnp.asarray(rotary_tables())
    hbm = pl.BlockSpec(memory_space=pl.ANY)
    vmem = pl.BlockSpec(memory_space=pltpu.VMEM)
    dma = pltpu.SemaphoreType.DMA
    projected, new_both = pl.pallas_call(
        kernel,
        out_shape=(
            jax.ShapeDtypeStruct((32, OUT_COLS), BF16),
            jax.ShapeDtypeStruct((2, NEW_DEV, HD), BF16),
        ),
        in_specs=[hbm] * 12,
        out_specs=(vmem, vmem),
        scratch_shapes=[
            pltpu.VMEM((NEW, FEAT), BF16),
            pltpu.VMEM((FEAT, 2 * HD), BF16),
            pltpu.VMEM((ROWS, HD), BF16),
            pltpu.VMEM((CACHED + SUFFIX, HD), BF16),
            pltpu.VMEM((CACHED + SUFFIX, HD), BF16),
            pltpu.VMEM((HD, CACHED + SUFFIX), BF16),
            pltpu.VMEM((2, GROUP * HALF, OUT_COLS), BF16),
            pltpu.VMEM((NEW_CHIP, 2 * HD), F32),
            pltpu.SMEM((1,), jnp.int32),
            pltpu.VMEM((1, 256), jnp.int32),
            pltpu.VMEM((PLANE, NEW_CHIP, HD), BF16),
            pltpu.VMEM((PLANE, NEW_CHIP, HD), BF16),
            pltpu.VMEM((PLANE, NEW_CHIP, HD), BF16),
            pltpu.VMEM((PLANE, NEW_CHIP, HD), BF16),
            pltpu.VMEM((NEW_CHIP, HD), F32),
            pltpu.VMEM((NEW_CHIP, HD), F32),
            pltpu.VMEM((NEW_DEV, HD), BF16),
            pltpu.VMEM((NEW_DEV, HD), BF16),
            pltpu.VMEM((NEW_DEV, HD), F32),
            pltpu.VMEM((PLANE, HD, CHUNK), F32),
            pltpu.VMEM((PLANE, 8, CHUNK), F32),
            pltpu.VMEM((PLANE, 8, CHUNK), F32),
            pltpu.VMEM((PLANE, FIRST, CHUNK), BF16),
            pltpu.VMEM((PLANE, FIRST, CHUNK), BF16),
            pltpu.VMEM((PLANE, HALF, CHUNK), BF16),
            pltpu.VMEM((PLANE, HALF, CHUNK), BF16),
            pltpu.VMEM((FIRST, CHUNK), BF16),
            pltpu.VMEM((FIRST, CHUNK), BF16),
            pltpu.VMEM((HALF, CHUNK), BF16),
            pltpu.VMEM((HALF, CHUNK), BF16),
            pltpu.VMEM((2, PLANE, HALF, HD), BF16),
            pltpu.VMEM((HEADS, 32, OUT_COLS), F32),
            pltpu.VMEM((HEADS, 32, OUT_COLS), BF16),
            pltpu.VMEM((HEADS, 32, OUT_COLS), BF16),
            dma((11,)),
            dma((2 * GROUP,)),
            dma((PLANE,)), dma((PLANE,)),
            dma, dma,
            dma((PLANE,)), dma((PLANE,)),
            dma, dma,
            dma((PLANE,)), dma((PLANE,)),
            dma((HEADS,)), dma((HEADS,)),
            dma((PLANE,)), dma((PLANE,)),
            dma, dma,
            dma((PLANE,)), dma((PLANE,)),
            dma, dma,
            dma((PLANE,)), dma((PLANE,)),
        ],
        compiler_params=pltpu.CompilerParams(
            collective_id=0, has_side_effects=True, vmem_limit_bytes=55168 * 1024
        ),
    )(
        queries.reshape(ROWS, HD),
        prefix_keys.reshape(CACHED, HD),
        prefix_values.reshape(CACHED, HD),
        new_states,
        key_weight,
        value_weight,
        suffix_keys.reshape(SUFFIX, HD),
        suffix_values.reshape(SUFFIX, HD),
        suffix_lengths,
        assignment.reshape(1, 256),
        out_weight,
        rot,
    )
    return (
        projected,
        new_both[0].reshape(NEW_DEV, 1, HD),
        new_both[1].reshape(NEW_DEV, 1, HD),
    )


def solution(mesh):
    in_specs = (
        P(None, "head", None),
        P(("ctx", "pool"), "head", None),
        P(("ctx", "pool"), "head", None),
        P(None, ("ctx", "pool")),
        P(("ctx", "pool"), "head"),
        P(("ctx", "pool"), "head"),
        P(("ctx", "pool"), None, "head", None),
        P(("ctx", "pool"), None, "head", None),
        P(("ctx", "pool")),
        P(),
        P("head", ("ctx", "pool")),
    )
    out_specs = (
        P("head", ("ctx", "pool")),
        P(("ctx", "pool"), "head", None),
        P(("ctx", "pool"), "head", None),
    )
    return jax.shard_map(body, mesh=mesh, in_specs=in_specs, out_specs=out_specs, check_vma=False)
```

```python
import functools
import math

import jax
import jax.numpy as jnp
import numpy as np
from jax import lax
from jax.experimental import pallas as pl
from jax.experimental.pallas import tpu as pltpu
from jax.sharding import PartitionSpec as P

F32 = jnp.float32
BF16 = jnp.bfloat16
NX = 4
PLANE = 16
POOL = 2
HEADS = 8
GROUP = 8
HD = 128
PREFIX = 8192
NEW = 1536
NEW_DEV = NEW // (PLANE * POOL)
NEW_CHIP = NEW_DEV * POOL
FEAT = 256
ROWS = 2048
CHUNK = 128
CACHED = 256
SUFFIX = 256
HALF = HD // 2
FIRST = HALF + 16
OUT_COLS = 256
SCALE = HD**-0.5 * math.log2(math.e)


def hops(i):
    return sum(min(d, NX - d) for d in (i % NX, i // NX))


FARTHEST = sorted(range(1, PLANE), key=lambda i: -hops(i))


def rotary_tables():
    half = HD // 2
    frequency = np.exp(
        np.arange(half, dtype=np.float32) * np.float32(-2.0 * math.log(500000.0) / HD)
    ).astype(np.float32)
    positions = (PREFIX + np.arange(NEW)).astype(np.float32)
    angles = (positions[:, None] * frequency[None, :]).astype(np.float32).astype(np.float64)
    cosine = np.cos(angles).astype(np.float32)
    sine = np.sin(angles).astype(np.float32)
    both = np.concatenate([cosine, cosine, -sine, sine], 1)
    return both.reshape(PLANE, NEW_CHIP, 2 * HD)


def mm(a, b, ca, cb):
    return lax.dot_general(a, b, (((ca,), (cb,)), ((), ())), preferred_element_type=F32)


def stat_rows(m, l):
    m1 = m.astype(BF16).astype(F32)
    r = m - m1
    m2 = r.astype(BF16).astype(F32)
    m3 = r - m2
    l1 = l.astype(BF16).astype(F32)
    r = l - l1
    l2 = r.astype(BF16).astype(F32)
    l3 = r - l2
    row = lax.broadcasted_iota(jnp.int32, (16, CHUNK), 0)
    out = jnp.zeros((16, CHUNK), F32)
    for k, part in enumerate((m1, m2, m3, l1, l2, l3)):
        out = jnp.where(row == k, jnp.broadcast_to(part, (16, CHUNK)), out)
    return out.astype(BF16)


def read_stats(tile):
    t = tile.astype(F32)
    m = (t[0:1] + t[1:2]) + t[2:3]
    l = (t[3:4] + t[4:5]) + t[5:6]
    return m, l


def kernel(
    q_hbm, pk_hbm, pv_hbm, st_hbm, kw_hbm, vw_hbm, sk_hbm, sv_hbm, len_hbm, asg_hbm, ow_hbm, rot_hbm,
    proj_ref, kv_ref,
    st_v, w_v, q_v, k_v, v_v, vt_v, ow_v, rot_v, len_v, asg_v,
    key_send, key_recv, val_send, val_recv, keyz_send, keyz_recv, valz_send, valz_recv, valz_kept,
    acc_v, m_v, l_v,
    low_send, low_recv, high_send, high_recv, lowz_send, lowz_recv, highz_send, highz_recv,
    ag_v, part_v, out_send, out_recv,
    lsem, wsem, s1, r1, s2, r2, s3, r3, s4, r4, s5, r5, s6, r6, s7, r7, s8, r8, s9, r9, s10, r10, s11, r11,
):
    c = lax.axis_index("ctx")
    h = lax.axis_index("head")
    p = lax.axis_index("pool")
    y = c // NX
    x = c % NX

    def plane_peer(i):
        return ((y + i // NX) % NX) * NX + (x + i % NX) % NX

    def remote(src, dst, ss, rs, cc, hh, pp):
        return pltpu.make_async_remote_copy(
            src_ref=src, dst_ref=dst, send_sem=ss, recv_sem=rs,
            device_id={"ctx": cc, "head": hh, "pool": pp},
            device_id_type=pl.DeviceIdType.MESH,
        )

    shard = c * POOL + p
    loads = [
        pltpu.make_async_copy(st_hbm, st_v, lsem.at[0]),
        pltpu.make_async_copy(kw_hbm, w_v.at[:, pl.ds(0, HD)], lsem.at[1]),
        pltpu.make_async_copy(vw_hbm, w_v.at[:, pl.ds(HD, HD)], lsem.at[2]),
        pltpu.make_async_copy(q_hbm, q_v, lsem.at[3]),
        pltpu.make_async_copy(pk_hbm, k_v.at[pl.ds(0, CACHED)], lsem.at[4]),
        pltpu.make_async_copy(sk_hbm, k_v.at[pl.ds(CACHED, SUFFIX)], lsem.at[5]),
        pltpu.make_async_copy(pv_hbm, v_v.at[pl.ds(0, CACHED)], lsem.at[6]),
        pltpu.make_async_copy(sv_hbm, v_v.at[pl.ds(CACHED, SUFFIX)], lsem.at[7]),
        pltpu.make_async_copy(rot_hbm.at[c], rot_v, lsem.at[8]),
        pltpu.make_async_copy(len_hbm, len_v, lsem.at[9]),
        pltpu.make_async_copy(asg_hbm, asg_v, lsem.at[10]),
    ]
    weights = [
        pltpu.make_async_copy(ow_hbm.at[:, f], ow_v.at[f], wsem.at[f]) for f in range(2)
    ]
    for copy in loads[:3]:
        copy.start()

    barrier = pltpu.get_barrier_semaphore()

    def greet(cc, hh, pp):
        pl.semaphore_signal(
            barrier, inc=1, device_id={"ctx": cc, "head": hh, "pool": pp},
            device_id_type=pl.DeviceIdType.MESH,
        )

    for i in FARTHEST:
        greet(plane_peer(i), h, p)
    greet(c, h, 1 - p)
    for j in range(1, HEADS):
        greet(c, (h + j) % HEADS, p)

    for copy in loads[:3]:
        copy.wait()

    for k in range(NX):
        rows = pl.ds(k * NX * NEW_CHIP, NX * NEW_CHIP)
        part = jnp.dot(st_v[rows, :], w_v[...], preferred_element_type=F32).astype(BF16)
        key_send[k * NX:(k + 1) * NX] = part[:, :HD].reshape(NX, NEW_CHIP, HD)
        val_send[k * NX:(k + 1) * NX] = part[:, HD:].reshape(NX, NEW_CHIP, HD)
    pl.semaphore_wait(barrier, (PLANE - 1) + 1 + (HEADS - 1))
    for i in FARTHEST:
        cc = plane_peer(i)
        remote(key_send.at[cc], key_recv.at[i], s1.at[i], r1.at[i], cc, h, p).start()
    for copy in loads[3:]:
        copy.start()

    for copy in weights:
        copy.start()

    def drain(src, dst, ss, rs):
        def left(i, carry):
            remote(src.at[c], dst.at[i], ss.at[i], rs.at[i], c, h, p).wait_send()
            return carry

        lax.fori_loop(1, PLANE, left, 0)

    for copy in loads[3:8] + loads[9:]:
        copy.wait()
    vt_v[...] = v_v[...].astype(F32).T.astype(BF16)
    suffix_id = shard
    lim = jnp.where(asg_v[...] == suffix_id, len_v[0], 0).astype(BF16)
    lim = jnp.broadcast_to(lim, (16, 256))

    def cached_block(b, carry):
        who = lax.broadcasted_iota(jnp.int32, (256, 256), 0)
        row = lax.broadcasted_iota(jnp.int32, (256, 256), 1)
        spread = jnp.where(who == b * 32 + row // GROUP, 1.0, 0.0).astype(BF16)
        lim_rows = mm(lim, spread, 1, 0)[0:1]
        qb = q_v[pl.ds(pl.multiple_of(b * 256, 256), 256), :]
        s = mm(k_v[...], qb, 1, 1) * SCALE
        key = lax.broadcasted_iota(jnp.int32, (SUFFIX, 256), 0).astype(F32)
        side = jnp.where(key < lim_rows, s[CACHED:], -jnp.inf)
        m = jnp.maximum(
            jnp.max(s[:CACHED], 0, keepdims=True), jnp.max(side, 0, keepdims=True)
        )
        main_e = jnp.exp2(s[:CACHED] - m)
        side_e = jnp.exp2(side - m)
        l = jnp.sum(main_e, 0, keepdims=True) + jnp.sum(side_e, 0, keepdims=True)
        e = jnp.concatenate([main_e.astype(BF16), side_e.astype(BF16)], 0)
        o = mm(vt_v[...], e, 1, 0)
        for k in range(2):
            lanes = slice(k * CHUNK, (k + 1) * CHUNK)
            acc_v[b * 2 + k] = o[:, lanes]
            m_v[b * 2 + k] = jnp.broadcast_to(m[:, lanes], (8, CHUNK))
            l_v[b * 2 + k] = jnp.broadcast_to(l[:, lanes], (8, CHUNK))
        return carry

    lax.fori_loop(0, 6, cached_block, 0, unroll=2)
    for i in FARTHEST:
        cc = plane_peer(i)
        remote(val_send.at[cc], val_recv.at[i], s7.at[i], r7.at[i], cc, h, p).start()
    lax.fori_loop(6, 8, cached_block, 0, unroll=2)

    mine = jnp.dot(
        st_v[pl.ds(pl.multiple_of(c * NEW_CHIP, NEW_CHIP), NEW_CHIP), :], w_v[...],
        preferred_element_type=F32,
    )

    def sum_keys(i, acc):
        remote(key_send.at[c], key_recv.at[i], s1.at[i], r1.at[i], c, h, p).wait_recv()
        return acc + key_recv[i].astype(F32)

    keyz_send[...] = lax.fori_loop(1, PLANE, sum_keys, mine[:, :HD])
    swap = remote(keyz_send, keyz_recv, s2, r2, c, h, 1 - p)
    swap.start()
    drain(key_send, key_recv, s1, r1)

    def sum_values(i, acc):
        remote(val_send.at[c], val_recv.at[i], s7.at[i], r7.at[i], c, h, p).wait_recv()
        return acc + val_recv[i].astype(F32)

    values = lax.fori_loop(1, PLANE, sum_values, mine[:, HD:])
    first = p == 0
    valz_send[...] = jnp.where(first, values[NEW_DEV:], values[:NEW_DEV]).astype(BF16)
    valz_kept[...] = jnp.where(first, values[:NEW_DEV], values[NEW_DEV:])
    swap_values = remote(valz_send, valz_recv, s8, r8, c, h, 1 - p)
    swap_values.start()
    new_vt = values.T.astype(BF16)
    loads[8].wait()
    swap.wait_recv()
    raw = keyz_send[...] + keyz_recv[...]
    turned = pltpu.roll(raw, HD // 2, 1)
    new_k = (raw * rot_v[:, :HD] + turned * rot_v[:, HD:]).astype(BF16)
    kv_ref[0] = jnp.where(first, new_k[:NEW_DEV], new_k[NEW_DEV:])
    token = lax.broadcasted_iota(jnp.int32, (NEW_CHIP, CHUNK), 0)
    counted = jnp.where((token // NEW_DEV) == p, 1.0, 0.0).astype(F32)

    def new_block(dy):
        yy = (y + dy) % NX
        qb = q_v[pl.ds(pl.multiple_of(yy * 512, 512), 512), :]
        s = mm(new_k, qb, 1, 1) * SCALE
        s_max = jnp.max(s, 0, keepdims=True)
        for k in range(NX):
            lanes = slice(k * CHUNK, (k + 1) * CHUNK)
            cc = yy * NX + k
            m_old = m_v[cc][0:1]
            m_new = jnp.maximum(m_old, s_max[:, lanes])
            shrink = jnp.exp2(m_old - m_new)
            e = jnp.exp2(s[:, lanes] - m_new)
            l_new = l_v[cc][0:1] * shrink + jnp.sum(e * counted, 0, keepdims=True)
            o = acc_v[cc] * shrink + mm(new_vt, e.astype(BF16), 1, 0)
            low_send[cc, 0:HALF] = o[:HALF].astype(BF16)
            low_send[cc, HALF:FIRST] = stat_rows(m_new, l_new)
            high_send[cc] = o[HALF:].astype(BF16)
            if dy == 0:
                acc_v[cc] = o
                m_v[cc] = jnp.broadcast_to(m_new, (8, CHUNK))
                l_v[cc] = jnp.broadcast_to(l_new, (8, CHUNK))

    for dy in (2, 1, 3, 0):
        new_block(dy)

        for dx in (2, 1, 3, 0):
            i = dy * NX + dx
            if i > 0:
                cc = plane_peer(i)
                remote(low_send.at[cc], low_recv.at[i], s3.at[i], r3.at[i], cc, h, p).start()
    for i in FARTHEST:
        cc = plane_peer(i)
        remote(low_send.at[cc], low_recv.at[i], s3.at[i], r3.at[i], cc, h, p).wait_send()
        remote(high_send.at[cc], high_recv.at[i], s9.at[i], r9.at[i], cc, h, p).start()

    drain(val_send, val_recv, s7, r7)
    swap.wait_send()

    def sum_low(i, state):
        remote(low_send.at[c], low_recv.at[i], s3.at[i], r3.at[i], c, h, p).wait_recv()
        acc, m, l = state
        m_in, l_in = read_stats(low_recv[i, HALF:FIRST])
        m_all = jnp.maximum(m, m_in)
        a = jnp.exp2(m - m_all)
        b = jnp.exp2(m_in - m_all)
        return (acc * a + low_recv[i, 0:HALF].astype(F32) * b, m_all, l * a + l_in * b)

    own_m = m_v[c][0:1]
    low, m, l = lax.fori_loop(1, PLANE, sum_low, (acc_v[c, 0:HALF], own_m, l_v[c][0:1]))
    lowz_send[0:HALF] = low.astype(BF16)
    lowz_send[HALF:FIRST] = stat_rows(m, l)
    swap_low = remote(lowz_send, lowz_recv, s4, r4, c, h, 1 - p)
    swap_low.start()

    def sum_high(i, acc):
        remote(high_send.at[c], high_recv.at[i], s9.at[i], r9.at[i], c, h, p).wait_recv()
        m_in, _ = read_stats(low_recv[i, HALF:FIRST])
        return acc + high_recv[i].astype(F32) * jnp.exp2(m_in - m)

    high = lax.fori_loop(1, PLANE, sum_high, acc_v[c, HALF:HD] * jnp.exp2(own_m - m))
    highz_send[...] = high.astype(BF16)
    swap_high = remote(highz_send, highz_recv, s10, r10, c, h, 1 - p)
    swap_high.start()

    to = lax.broadcasted_iota(jnp.int32, (HALF, CHUNK), 0)
    frm = lax.broadcasted_iota(jnp.int32, (HALF, CHUNK), 1)
    perms = [
        jnp.where(frm == (to % 16) * GROUP + (to // 16) * 2 + k, 1.0, 0.0).astype(BF16)
        for k in range(2)
    ]
    drain(high_send, high_recv, s9, r9)

    swap_low.wait_recv()
    m_in, l_in = read_stats(lowz_recv[HALF:FIRST])
    m_all = jnp.maximum(m, m_in)
    a = jnp.exp2(m - m_all)
    b = jnp.exp2(m_in - m_all)
    inverse = 1.0 / (l * a + l_in * b)
    a, b = a * inverse, b * inverse

    def share(f, mine, other, ss, rs):
        att = (mine * a + other.astype(F32) * b).astype(BF16)
        ag_v[f, c] = jnp.concatenate([mm(perm, att, 1, 1) for perm in perms], 1).astype(BF16)
        for i in FARTHEST:
            remote(ag_v.at[f, c], ag_v.at[f, c], ss.at[i], rs.at[i], plane_peer(i), h, p).start()

    share(0, low, lowz_recv[0:HALF], s5, r5)
    swap_high.wait_recv()
    share(1, high, highz_recv[...], s11, r11)
    swap_values.wait_recv()
    kv_ref[1] = (valz_kept[...] + valz_recv[...].astype(F32)).astype(BF16)
    swap_values.wait_send()
    swap_low.wait_send()
    swap_high.wait_send()
    for copy in weights:
        copy.wait()

    def product(f, yy, dy, ss, rs):
        for dx in range(NX):
            i = dy * NX + dx
            if i > 0:
                src = yy * NX + (x + NX - dx) % NX
                remote(ag_v.at[f, c], ag_v.at[f, src], ss.at[i], rs.at[i], c, h, p).wait_recv()
        rows = ag_v[f, pl.ds(yy * NX, NX)]
        rows = jnp.concatenate(
            [rows[:, k * 16:(k + 1) * 16, :].reshape(NX * 16, HD) for k in range(GROUP // 2)], 1
        )
        return jnp.dot(rows, ow_v[f].reshape(GROUP * HALF, OUT_COLS), preferred_element_type=F32)

    for dy in (0, 1, 3, 2):
        yy = (y + NX - dy) % NX
        part_v[pl.ds(yy * 2, 2)] = product(0, yy, dy, s5, r5).reshape(2, 32, OUT_COLS)
    for dy in (0, 1, 3, 2):
        yy = (y + NX - dy) % NX
        out = part_v[pl.ds(yy * 2, 2)].reshape(NX * 16, OUT_COLS) + product(1, yy, dy, s11, r11)
        part_v[pl.ds(yy * 2, 2)] = out.reshape(2, 32, OUT_COLS)
        out_send[pl.ds(yy * 2, 2)] = out.astype(BF16).reshape(2, 32, OUT_COLS)
        for k in range(2):
            hh = yy * 2 + k
            j = (hh + HEADS - h) % HEADS

            @pl.when(j != 0)
            def _():
                remote(out_send.at[hh], out_recv.at[j], s6.at[j], r6.at[j], c, hh, p).start()

    def left_ag(i, carry):
        remote(ag_v.at[0, c], ag_v.at[0, c], s5.at[i], r5.at[i], c, h, p).wait_send()
        remote(ag_v.at[1, c], ag_v.at[1, c], s11.at[i], r11.at[i], c, h, p).wait_send()
        return carry

    lax.fori_loop(1, PLANE, left_ag, 0)

    def sum_out(j, acc):
        remote(out_send.at[h], out_recv.at[j], s6.at[j], r6.at[j], c, h, p).wait_recv()
        return acc + out_recv[j].astype(F32)

    proj_ref[...] = lax.fori_loop(1, HEADS, sum_out, part_v[h]).astype(BF16)

    def left_out(j, carry):
        remote(out_send.at[h], out_recv.at[j], s6.at[j], r6.at[j], c, h, p).wait_send()
        return carry

    lax.fori_loop(1, HEADS, left_out, 0)


def body(
    queries, prefix_keys, prefix_values, new_states, key_weight, value_weight,
    suffix_keys, suffix_values, suffix_lengths, assignment, out_weight,
):
    rot = jnp.asarray(rotary_tables())
    hbm = pl.BlockSpec(memory_space=pl.ANY)
    vmem = pl.BlockSpec(memory_space=pltpu.VMEM)
    dma = pltpu.SemaphoreType.DMA
    projected, new_both = pl.pallas_call(
        kernel,
        out_shape=(
            jax.ShapeDtypeStruct((32, OUT_COLS), BF16),
            jax.ShapeDtypeStruct((2, NEW_DEV, HD), BF16),
        ),
        in_specs=[hbm] * 12,
        out_specs=(vmem, vmem),
        scratch_shapes=[
            pltpu.VMEM((NEW, FEAT), BF16),
            pltpu.VMEM((FEAT, 2 * HD), BF16),
            pltpu.VMEM((ROWS, HD), BF16),
            pltpu.VMEM((CACHED + SUFFIX, HD), BF16),
            pltpu.VMEM((CACHED + SUFFIX, HD), BF16),
            pltpu.VMEM((HD, CACHED + SUFFIX), BF16),
            pltpu.VMEM((2, GROUP, HALF, OUT_COLS), BF16),
            pltpu.VMEM((NEW_CHIP, 2 * HD), F32),
            pltpu.SMEM((1,), jnp.int32),
            pltpu.VMEM((1, 256), jnp.int32),
            pltpu.VMEM((PLANE, NEW_CHIP, HD), BF16),
            pltpu.VMEM((PLANE, NEW_CHIP, HD), BF16),
            pltpu.VMEM((PLANE, NEW_CHIP, HD), BF16),
            pltpu.VMEM((PLANE, NEW_CHIP, HD), BF16),
            pltpu.VMEM((NEW_CHIP, HD), F32),
            pltpu.VMEM((NEW_CHIP, HD), F32),
            pltpu.VMEM((NEW_DEV, HD), BF16),
            pltpu.VMEM((NEW_DEV, HD), BF16),
            pltpu.VMEM((NEW_DEV, HD), F32),
            pltpu.VMEM((PLANE, HD, CHUNK), F32),
            pltpu.VMEM((PLANE, 8, CHUNK), F32),
            pltpu.VMEM((PLANE, 8, CHUNK), F32),
            pltpu.VMEM((PLANE, FIRST, CHUNK), BF16),
            pltpu.VMEM((PLANE, FIRST, CHUNK), BF16),
            pltpu.VMEM((PLANE, HALF, CHUNK), BF16),
            pltpu.VMEM((PLANE, HALF, CHUNK), BF16),
            pltpu.VMEM((FIRST, CHUNK), BF16),
            pltpu.VMEM((FIRST, CHUNK), BF16),
            pltpu.VMEM((HALF, CHUNK), BF16),
            pltpu.VMEM((HALF, CHUNK), BF16),
            pltpu.VMEM((2, PLANE, HALF, HD), BF16),
            pltpu.VMEM((HEADS, 32, OUT_COLS), F32),
            pltpu.VMEM((HEADS, 32, OUT_COLS), BF16),
            pltpu.VMEM((HEADS, 32, OUT_COLS), BF16),
            dma((11,)),
            dma((2,)),
            dma((PLANE,)), dma((PLANE,)),
            dma, dma,
            dma((PLANE,)), dma((PLANE,)),
            dma, dma,
            dma((PLANE,)), dma((PLANE,)),
            dma((HEADS,)), dma((HEADS,)),
            dma((PLANE,)), dma((PLANE,)),
            dma, dma,
            dma((PLANE,)), dma((PLANE,)),
            dma, dma,
            dma((PLANE,)), dma((PLANE,)),
        ],
        compiler_params=pltpu.CompilerParams(
            collective_id=0, has_side_effects=True, vmem_limit_bytes=55168 * 1024
        ),
    )(
        queries.reshape(ROWS, HD),
        prefix_keys.reshape(CACHED, HD),
        prefix_values.reshape(CACHED, HD),
        new_states,
        key_weight,
        value_weight,
        suffix_keys.reshape(SUFFIX, HD),
        suffix_values.reshape(SUFFIX, HD),
        suffix_lengths,
        assignment.reshape(1, 256),
        out_weight.reshape(GROUP, 2, HALF, OUT_COLS),
        rot,
    )
    return (
        projected,
        new_both[0].reshape(NEW_DEV, 1, HD),
        new_both[1].reshape(NEW_DEV, 1, HD),
    )


def solution(mesh):
    in_specs = (
        P(None, "head", None),
        P(("ctx", "pool"), "head", None),
        P(("ctx", "pool"), "head", None),
        P(None, ("ctx", "pool")),
        P(("ctx", "pool"), "head"),
        P(("ctx", "pool"), "head"),
        P(("ctx", "pool"), None, "head", None),
        P(("ctx", "pool"), None, "head", None),
        P(("ctx", "pool")),
        P(),
        P("head", ("ctx", "pool")),
    )
    out_specs = (
        P("head", ("ctx", "pool")),
        P(("ctx", "pool"), "head", None),
        P(("ctx", "pool"), "head", None),
    )
    return jax.shard_map(body, mesh=mesh, in_specs=in_specs, out_specs=out_specs, check_vma=False)
```

```python
import functools
import math

import jax
import jax.numpy as jnp
import numpy as np
from jax import lax
from jax.experimental import pallas as pl
from jax.experimental.pallas import tpu as pltpu
from jax.sharding import PartitionSpec as P

F32 = jnp.float32
BF16 = jnp.bfloat16
NX = 4
PLANE = 16
POOL = 2
HEADS = 8
GROUP = 8
HD = 128
PREFIX = 8192
NEW = 1536
NEW_DEV = NEW // (PLANE * POOL)
NEW_CHIP = NEW_DEV * POOL
FEAT = 256
ROWS = 2048
CHUNK = 128
CACHED = 256
SUFFIX = 256
HALF = HD // 2
FIRST = HALF + 16
OUT_COLS = 256
SCALE = HD**-0.5 * math.log2(math.e)


def hops(i):
    return sum(min(d, NX - d) for d in (i % NX, i // NX))


FARTHEST = sorted(range(1, PLANE), key=lambda i: -hops(i))


def rotary_tables():
    half = HD // 2
    frequency = np.exp(
        np.arange(half, dtype=np.float32) * np.float32(-2.0 * math.log(500000.0) / HD)
    ).astype(np.float32)
    positions = (PREFIX + np.arange(NEW)).astype(np.float32)
    angles = (positions[:, None] * frequency[None, :]).astype(np.float32).astype(np.float64)
    cosine = np.cos(angles).astype(np.float32)
    sine = np.sin(angles).astype(np.float32)
    both = np.concatenate([cosine, cosine, -sine, sine], 1)
    return both.reshape(PLANE, NEW_CHIP, 2 * HD)


def mm(a, b, ca, cb):
    return lax.dot_general(a, b, (((ca,), (cb,)), ((), ())), preferred_element_type=F32)


def stat_rows(m, l):
    m1 = m.astype(BF16).astype(F32)
    r = m - m1
    m2 = r.astype(BF16).astype(F32)
    m3 = r - m2
    l1 = l.astype(BF16).astype(F32)
    r = l - l1
    l2 = r.astype(BF16).astype(F32)
    l3 = r - l2
    row = lax.broadcasted_iota(jnp.int32, (16, CHUNK), 0)
    out = jnp.zeros((16, CHUNK), F32)
    for k, part in enumerate((m1, m2, m3, l1, l2, l3)):
        out = jnp.where(row == k, jnp.broadcast_to(part, (16, CHUNK)), out)
    return out.astype(BF16)


def read_stats(tile):
    t = tile.astype(F32)
    m = (t[0:1] + t[1:2]) + t[2:3]
    l = (t[3:4] + t[4:5]) + t[5:6]
    return m, l


def kernel(
    q_hbm, pk_hbm, pv_hbm, st_hbm, kw_hbm, vw_hbm, sk_hbm, sv_hbm, len_hbm, asg_hbm, ow_hbm, rot_hbm,
    proj_ref, kv_ref,
    st_v, w_v, q_v, k_v, v_v, vt_v, ow_v, rot_v, len_v, asg_v,
    key_send, key_recv, val_send, val_recv, keyz_send, keyz_recv, valz_send, valz_recv, valz_kept,
    acc_v, m_v, l_v,
    low_send, low_recv, high_send, high_recv, lowz_send, lowz_recv, highz_send, highz_recv,
    ag_v, part_v, out_send, out_recv,
    lsem, wsem, s1, r1, s2, r2, s3, r3, s4, r4, s5, r5, s6, r6, s7, r7, s8, r8, s9, r9, s10, r10, s11, r11,
):
    c = lax.axis_index("ctx")
    h = lax.axis_index("head")
    p = lax.axis_index("pool")
    y = c // NX
    x = c % NX

    def plane_peer(i):
        return ((y + i // NX) % NX) * NX + (x + i % NX) % NX

    def remote(src, dst, ss, rs, cc, hh, pp):
        return pltpu.make_async_remote_copy(
            src_ref=src, dst_ref=dst, send_sem=ss, recv_sem=rs,
            device_id={"ctx": cc, "head": hh, "pool": pp},
            device_id_type=pl.DeviceIdType.MESH,
        )

    shard = c * POOL + p
    loads = [
        pltpu.make_async_copy(st_hbm, st_v, lsem.at[0]),
        pltpu.make_async_copy(kw_hbm, w_v.at[:, pl.ds(0, HD)], lsem.at[1]),
        pltpu.make_async_copy(vw_hbm, w_v.at[:, pl.ds(HD, HD)], lsem.at[2]),
        pltpu.make_async_copy(q_hbm, q_v, lsem.at[3]),
        pltpu.make_async_copy(pk_hbm, k_v.at[pl.ds(0, CACHED)], lsem.at[4]),
        pltpu.make_async_copy(sk_hbm, k_v.at[pl.ds(CACHED, SUFFIX)], lsem.at[5]),
        pltpu.make_async_copy(pv_hbm, v_v.at[pl.ds(0, CACHED)], lsem.at[6]),
        pltpu.make_async_copy(sv_hbm, v_v.at[pl.ds(CACHED, SUFFIX)], lsem.at[7]),
        pltpu.make_async_copy(rot_hbm.at[c], rot_v, lsem.at[8]),
        pltpu.make_async_copy(len_hbm, len_v, lsem.at[9]),
        pltpu.make_async_copy(asg_hbm, asg_v, lsem.at[10]),
    ]
    weights = [
        pltpu.make_async_copy(ow_hbm.at[:, f], ow_v.at[f], wsem.at[f]) for f in range(2)
    ]
    for copy in loads[:3]:
        copy.start()

    barrier = pltpu.get_barrier_semaphore()

    def greet(cc, hh, pp):
        pl.semaphore_signal(
            barrier, inc=1, device_id={"ctx": cc, "head": hh, "pool": pp},
            device_id_type=pl.DeviceIdType.MESH,
        )

    for i in FARTHEST:
        greet(plane_peer(i), h, p)
    greet(c, h, 1 - p)
    for j in range(1, HEADS):
        greet(c, (h + j) % HEADS, p)

    for copy in loads[:3]:
        copy.wait()

    for k in range(NX):
        rows = pl.ds(k * NX * NEW_CHIP, NX * NEW_CHIP)
        part = jnp.dot(st_v[rows, :], w_v[...], preferred_element_type=F32).astype(BF16)
        key_send[k * NX:(k + 1) * NX] = part[:, :HD].reshape(NX, NEW_CHIP, HD)
        val_send[k * NX:(k + 1) * NX] = part[:, HD:].reshape(NX, NEW_CHIP, HD)
    pl.semaphore_wait(barrier, (PLANE - 1) + 1 + (HEADS - 1))
    for i in FARTHEST:
        cc = plane_peer(i)
        remote(key_send.at[cc], key_recv.at[i], s1.at[i], r1.at[i], cc, h, p).start()
    for copy in loads[3:]:
        copy.start()

    for copy in weights:
        copy.start()

    def drain(src, dst, ss, rs):
        def left(i, carry):
            remote(src.at[c], dst.at[i], ss.at[i], rs.at[i], c, h, p).wait_send()
            return carry

        lax.fori_loop(1, PLANE, left, 0)

    for copy in loads[3:8] + loads[9:]:
        copy.wait()
    vt_v[...] = v_v[...].astype(F32).T.astype(BF16)
    suffix_id = shard
    lim = jnp.where(asg_v[...] == suffix_id, len_v[0], 0).astype(BF16)
    lim = jnp.broadcast_to(lim, (16, 256))

    def cached_block(b, carry):
        who = lax.broadcasted_iota(jnp.int32, (256, 256), 0)
        row = lax.broadcasted_iota(jnp.int32, (256, 256), 1)
        spread = jnp.where(who == b * 32 + row // GROUP, 1.0, 0.0).astype(BF16)
        lim_rows = mm(lim, spread, 1, 0)[0:1]
        qb = q_v[pl.ds(pl.multiple_of(b * 256, 256), 256), :]
        s = mm(k_v[...], qb, 1, 1) * SCALE
        key = lax.broadcasted_iota(jnp.int32, (SUFFIX, 256), 0).astype(F32)
        side = jnp.where(key < lim_rows, s[CACHED:], -jnp.inf)
        m = jnp.maximum(
            jnp.max(s[:CACHED], 0, keepdims=True), jnp.max(side, 0, keepdims=True)
        )
        main_e = jnp.exp2(s[:CACHED] - m)
        side_e = jnp.exp2(side - m)
        l = jnp.sum(main_e, 0, keepdims=True) + jnp.sum(side_e, 0, keepdims=True)
        e = jnp.concatenate([main_e.astype(BF16), side_e.astype(BF16)], 0)
        o = mm(vt_v[...], e, 1, 0)
        for k in range(2):
            lanes = slice(k * CHUNK, (k + 1) * CHUNK)
            acc_v[b * 2 + k] = o[:, lanes]
            m_v[b * 2 + k] = jnp.broadcast_to(m[:, lanes], (8, CHUNK))
            l_v[b * 2 + k] = jnp.broadcast_to(l[:, lanes], (8, CHUNK))
        return carry

    lax.fori_loop(0, 6, cached_block, 0, unroll=3)
    for i in FARTHEST:
        cc = plane_peer(i)
        remote(val_send.at[cc], val_recv.at[i], s7.at[i], r7.at[i], cc, h, p).start()
    lax.fori_loop(6, 8, cached_block, 0, unroll=2)

    mine = jnp.dot(
        st_v[pl.ds(pl.multiple_of(c * NEW_CHIP, NEW_CHIP), NEW_CHIP), :], w_v[...],
        preferred_element_type=F32,
    )

    def sum_keys(i, acc):
        remote(key_send.at[c], key_recv.at[i], s1.at[i], r1.at[i], c, h, p).wait_recv()
        return acc + key_recv[i].astype(F32)

    keyz_send[...] = lax.fori_loop(1, PLANE, sum_keys, mine[:, :HD])
    swap = remote(keyz_send, keyz_recv, s2, r2, c, h, 1 - p)
    swap.start()
    drain(key_send, key_recv, s1, r1)

    def sum_values(i, acc):
        remote(val_send.at[c], val_recv.at[i], s7.at[i], r7.at[i], c, h, p).wait_recv()
        return acc + val_recv[i].astype(F32)

    values = lax.fori_loop(1, PLANE, sum_values, mine[:, HD:])
    first = p == 0
    valz_send[...] = jnp.where(first, values[NEW_DEV:], values[:NEW_DEV]).astype(BF16)
    valz_kept[...] = jnp.where(first, values[:NEW_DEV], values[NEW_DEV:])
    swap_values = remote(valz_send, valz_recv, s8, r8, c, h, 1 - p)
    swap_values.start()
    new_vt = values.T.astype(BF16)
    loads[8].wait()
    swap.wait_recv()
    raw = keyz_send[...] + keyz_recv[...]
    turned = pltpu.roll(raw, HD // 2, 1)
    new_k = (raw * rot_v[:, :HD] + turned * rot_v[:, HD:]).astype(BF16)
    kv_ref[0] = jnp.where(first, new_k[:NEW_DEV], new_k[NEW_DEV:])
    token = lax.broadcasted_iota(jnp.int32, (NEW_CHIP, CHUNK), 0)
    counted = jnp.where((token // NEW_DEV) == p, 1.0, 0.0).astype(F32)

    def new_block(dy):
        yy = (y + dy) % NX
        qb = q_v[pl.ds(pl.multiple_of(yy * 512, 512), 512), :]
        s = mm(new_k, qb, 1, 1) * SCALE
        s_max = jnp.max(s, 0, keepdims=True)
        for k in range(NX):
            lanes = slice(k * CHUNK, (k + 1) * CHUNK)
            cc = yy * NX + k
            m_old = m_v[cc][0:1]
            m_new = jnp.maximum(m_old, s_max[:, lanes])
            shrink = jnp.exp2(m_old - m_new)
            e = jnp.exp2(s[:, lanes] - m_new)
            l_new = l_v[cc][0:1] * shrink + jnp.sum(e * counted, 0, keepdims=True)
            o = acc_v[cc] * shrink + mm(new_vt, e.astype(BF16), 1, 0)
            low_send[cc, 0:HALF] = o[:HALF].astype(BF16)
            low_send[cc, HALF:FIRST] = stat_rows(m_new, l_new)
            high_send[cc] = o[HALF:].astype(BF16)
            if dy == 0:
                acc_v[cc] = o
                m_v[cc] = jnp.broadcast_to(m_new, (8, CHUNK))
                l_v[cc] = jnp.broadcast_to(l_new, (8, CHUNK))

    for dy in (2, 1, 3, 0):
        new_block(dy)

        for dx in (2, 1, 3, 0):
            i = dy * NX + dx
            if i > 0:
                cc = plane_peer(i)
                remote(low_send.at[cc], low_recv.at[i], s3.at[i], r3.at[i], cc, h, p).start()
    for i in FARTHEST:
        cc = plane_peer(i)
        remote(low_send.at[cc], low_recv.at[i], s3.at[i], r3.at[i], cc, h, p).wait_send()
        remote(high_send.at[cc], high_recv.at[i], s9.at[i], r9.at[i], cc, h, p).start()

    drain(val_send, val_recv, s7, r7)
    swap.wait_send()

    own_m = m_v[c][0:1]


    def largest(i, m):
        remote(low_send.at[c], low_recv.at[i], s3.at[i], r3.at[i], c, h, p).wait_recv()
        return jnp.maximum(m, read_stats(low_recv[i, HALF:FIRST])[0])

    m = lax.fori_loop(1, PLANE, largest, own_m)

    def sum_low(i, state):
        m_in, l_in = read_stats(low_recv[i, HALF:FIRST])
        b = jnp.exp2(m_in - m)
        return (state[0] + low_recv[i, 0:HALF].astype(F32) * b, state[1] + l_in * b)

    a = jnp.exp2(own_m - m)
    low, l = lax.fori_loop(
        1, PLANE, sum_low, (acc_v[c, 0:HALF] * a, l_v[c][0:1] * a), unroll=5
    )
    lowz_send[0:HALF] = low.astype(BF16)
    lowz_send[HALF:FIRST] = stat_rows(m, l)
    swap_low = remote(lowz_send, lowz_recv, s4, r4, c, h, 1 - p)
    swap_low.start()

    def sum_high(i, acc):
        remote(high_send.at[c], high_recv.at[i], s9.at[i], r9.at[i], c, h, p).wait_recv()
        m_in, _ = read_stats(low_recv[i, HALF:FIRST])
        return acc + high_recv[i].astype(F32) * jnp.exp2(m_in - m)

    high = lax.fori_loop(1, PLANE, sum_high, acc_v[c, HALF:HD] * jnp.exp2(own_m - m), unroll=5)
    highz_send[...] = high.astype(BF16)
    swap_high = remote(highz_send, highz_recv, s10, r10, c, h, 1 - p)
    swap_high.start()

    to = lax.broadcasted_iota(jnp.int32, (HALF, CHUNK), 0)
    frm = lax.broadcasted_iota(jnp.int32, (HALF, CHUNK), 1)
    perms = [
        jnp.where(frm == (to % 16) * GROUP + (to // 16) * 2 + k, 1.0, 0.0).astype(BF16)
        for k in range(2)
    ]
    drain(high_send, high_recv, s9, r9)

    swap_low.wait_recv()
    m_in, l_in = read_stats(lowz_recv[HALF:FIRST])
    m_all = jnp.maximum(m, m_in)
    a = jnp.exp2(m - m_all)
    b = jnp.exp2(m_in - m_all)
    inverse = 1.0 / (l * a + l_in * b)
    a, b = a * inverse, b * inverse

    def share(f, mine, other, ss, rs):
        att = (mine * a + other.astype(F32) * b).astype(BF16)
        ag_v[f, c] = jnp.concatenate([mm(perm, att, 1, 1) for perm in perms], 1).astype(BF16)
        for i in FARTHEST:
            remote(ag_v.at[f, c], ag_v.at[f, c], ss.at[i], rs.at[i], plane_peer(i), h, p).start()

    share(0, low, lowz_recv[0:HALF], s5, r5)
    swap_high.wait_recv()
    share(1, high, highz_recv[...], s11, r11)
    swap_values.wait_recv()
    kv_ref[1] = (valz_kept[...] + valz_recv[...].astype(F32)).astype(BF16)
    swap_values.wait_send()
    swap_low.wait_send()
    swap_high.wait_send()
    for copy in weights:
        copy.wait()

    def product(f, yy, dy, ss, rs):
        for dx in range(NX):
            i = dy * NX + dx
            if i > 0:
                src = yy * NX + (x + NX - dx) % NX
                remote(ag_v.at[f, c], ag_v.at[f, src], ss.at[i], rs.at[i], c, h, p).wait_recv()
        rows = ag_v[f, pl.ds(yy * NX, NX)]
        rows = jnp.concatenate(
            [rows[:, k * 16:(k + 1) * 16, :].reshape(NX * 16, HD) for k in range(GROUP // 2)], 1
        )
        return jnp.dot(rows, ow_v[f].reshape(GROUP * HALF, OUT_COLS), preferred_element_type=F32)

    for dy in (0, 1, 3, 2):
        yy = (y + NX - dy) % NX
        part_v[pl.ds(yy * 2, 2)] = product(0, yy, dy, s5, r5).reshape(2, 32, OUT_COLS)
    for dy in (0, 1, 3, 2):
        yy = (y + NX - dy) % NX
        out = part_v[pl.ds(yy * 2, 2)].reshape(NX * 16, OUT_COLS) + product(1, yy, dy, s11, r11)
        part_v[pl.ds(yy * 2, 2)] = out.reshape(2, 32, OUT_COLS)
        out_send[pl.ds(yy * 2, 2)] = out.astype(BF16).reshape(2, 32, OUT_COLS)
        for k in range(2):
            hh = yy * 2 + k
            j = (hh + HEADS - h) % HEADS

            @pl.when(j != 0)
            def _():
                remote(out_send.at[hh], out_recv.at[j], s6.at[j], r6.at[j], c, hh, p).start()

    def left_ag(i, carry):
        remote(ag_v.at[0, c], ag_v.at[0, c], s5.at[i], r5.at[i], c, h, p).wait_send()
        remote(ag_v.at[1, c], ag_v.at[1, c], s11.at[i], r11.at[i], c, h, p).wait_send()
        return carry

    lax.fori_loop(1, PLANE, left_ag, 0)

    def sum_out(j, acc):
        remote(out_send.at[h], out_recv.at[j], s6.at[j], r6.at[j], c, h, p).wait_recv()
        return acc + out_recv[j].astype(F32)

    proj_ref[...] = lax.fori_loop(1, HEADS, sum_out, part_v[h], unroll=True).astype(BF16)

    def left_out(j, carry):
        remote(out_send.at[h], out_recv.at[j], s6.at[j], r6.at[j], c, h, p).wait_send()
        return carry

    lax.fori_loop(1, HEADS, left_out, 0)


def body(
    queries, prefix_keys, prefix_values, new_states, key_weight, value_weight,
    suffix_keys, suffix_values, suffix_lengths, assignment, out_weight,
):
    rot = jnp.asarray(rotary_tables())
    hbm = pl.BlockSpec(memory_space=pl.ANY)
    vmem = pl.BlockSpec(memory_space=pltpu.VMEM)
    dma = pltpu.SemaphoreType.DMA
    projected, new_both = pl.pallas_call(
        kernel,
        out_shape=(
            jax.ShapeDtypeStruct((32, OUT_COLS), BF16),
            jax.ShapeDtypeStruct((2, NEW_DEV, HD), BF16),
        ),
        in_specs=[hbm] * 12,
        out_specs=(vmem, vmem),
        scratch_shapes=[
            pltpu.VMEM((NEW, FEAT), BF16),
            pltpu.VMEM((FEAT, 2 * HD), BF16),
            pltpu.VMEM((ROWS, HD), BF16),
            pltpu.VMEM((CACHED + SUFFIX, HD), BF16),
            pltpu.VMEM((CACHED + SUFFIX, HD), BF16),
            pltpu.VMEM((HD, CACHED + SUFFIX), BF16),
            pltpu.VMEM((2, GROUP, HALF, OUT_COLS), BF16),
            pltpu.VMEM((NEW_CHIP, 2 * HD), F32),
            pltpu.SMEM((1,), jnp.int32),
            pltpu.VMEM((1, 256), jnp.int32),
            pltpu.VMEM((PLANE, NEW_CHIP, HD), BF16),
            pltpu.VMEM((PLANE, NEW_CHIP, HD), BF16),
            pltpu.VMEM((PLANE, NEW_CHIP, HD), BF16),
            pltpu.VMEM((PLANE, NEW_CHIP, HD), BF16),
            pltpu.VMEM((NEW_CHIP, HD), F32),
            pltpu.VMEM((NEW_CHIP, HD), F32),
            pltpu.VMEM((NEW_DEV, HD), BF16),
            pltpu.VMEM((NEW_DEV, HD), BF16),
            pltpu.VMEM((NEW_DEV, HD), F32),
            pltpu.VMEM((PLANE, HD, CHUNK), F32),
            pltpu.VMEM((PLANE, 8, CHUNK), F32),
            pltpu.VMEM((PLANE, 8, CHUNK), F32),
            pltpu.VMEM((PLANE, FIRST, CHUNK), BF16),
            pltpu.VMEM((PLANE, FIRST, CHUNK), BF16),
            pltpu.VMEM((PLANE, HALF, CHUNK), BF16),
            pltpu.VMEM((PLANE, HALF, CHUNK), BF16),
            pltpu.VMEM((FIRST, CHUNK), BF16),
            pltpu.VMEM((FIRST, CHUNK), BF16),
            pltpu.VMEM((HALF, CHUNK), BF16),
            pltpu.VMEM((HALF, CHUNK), BF16),
            pltpu.VMEM((2, PLANE, HALF, HD), BF16),
            pltpu.VMEM((HEADS, 32, OUT_COLS), F32),
            pltpu.VMEM((HEADS, 32, OUT_COLS), BF16),
            pltpu.VMEM((HEADS, 32, OUT_COLS), BF16),
            dma((11,)),
            dma((2,)),
            dma((PLANE,)), dma((PLANE,)),
            dma, dma,
            dma((PLANE,)), dma((PLANE,)),
            dma, dma,
            dma((PLANE,)), dma((PLANE,)),
            dma((HEADS,)), dma((HEADS,)),
            dma((PLANE,)), dma((PLANE,)),
            dma, dma,
            dma((PLANE,)), dma((PLANE,)),
            dma, dma,
            dma((PLANE,)), dma((PLANE,)),
        ],
        compiler_params=pltpu.CompilerParams(
            collective_id=0, has_side_effects=True, vmem_limit_bytes=55168 * 1024
        ),
    )(
        queries.reshape(ROWS, HD),
        prefix_keys.reshape(CACHED, HD),
        prefix_values.reshape(CACHED, HD),
        new_states,
        key_weight,
        value_weight,
        suffix_keys.reshape(SUFFIX, HD),
        suffix_values.reshape(SUFFIX, HD),
        suffix_lengths,
        assignment.reshape(1, 256),
        out_weight.reshape(GROUP, 2, HALF, OUT_COLS),
        rot,
    )
    return (
        projected,
        new_both[0].reshape(NEW_DEV, 1, HD),
        new_both[1].reshape(NEW_DEV, 1, HD),
    )


def solution(mesh):
    in_specs = (
        P(None, "head", None),
        P(("ctx", "pool"), "head", None),
        P(("ctx", "pool"), "head", None),
        P(None, ("ctx", "pool")),
        P(("ctx", "pool"), "head"),
        P(("ctx", "pool"), "head"),
        P(("ctx", "pool"), None, "head", None),
        P(("ctx", "pool"), None, "head", None),
        P(("ctx", "pool")),
        P(),
        P("head", ("ctx", "pool")),
    )
    out_specs = (
        P("head", ("ctx", "pool")),
        P(("ctx", "pool"), "head", None),
        P(("ctx", "pool"), "head", None),
    )
    return jax.shard_map(body, mesh=mesh, in_specs=in_specs, out_specs=out_specs, check_vma=False)
```

```python
import functools
import math

import jax
import jax.numpy as jnp
import numpy as np
from jax import lax
from jax.experimental import pallas as pl
from jax.experimental.pallas import tpu as pltpu
from jax.sharding import PartitionSpec as P

F32 = jnp.float32
BF16 = jnp.bfloat16
NX = 4
PLANE = 16
POOL = 2
HEADS = 8
GROUP = 8
HD = 128
PREFIX = 8192
NEW = 1536
NEW_DEV = NEW // (PLANE * POOL)
NEW_CHIP = NEW_DEV * POOL
FEAT = 256
ROWS = 2048
CHUNK = 128
CACHED = 256
SUFFIX = 256
HALF = HD // 2
FIRST = HALF + 16
OUT_COLS = 256
SCALE = HD**-0.5 * math.log2(math.e)


def hops(i):
    return sum(min(d, NX - d) for d in (i % NX, i // NX))


FARTHEST = sorted(range(1, PLANE), key=lambda i: -hops(i))


def rotary_tables():
    half = HD // 2
    frequency = np.exp(
        np.arange(half, dtype=np.float32) * np.float32(-2.0 * math.log(500000.0) / HD)
    ).astype(np.float32)
    positions = (PREFIX + np.arange(NEW)).astype(np.float32)
    angles = (positions[:, None] * frequency[None, :]).astype(np.float32).astype(np.float64)
    cosine = np.cos(angles).astype(np.float32)
    sine = np.sin(angles).astype(np.float32)
    both = np.concatenate([cosine, cosine, -sine, sine], 1)
    return both.reshape(PLANE, NEW_CHIP, 2 * HD)


def mm(a, b, ca, cb):
    return lax.dot_general(a, b, (((ca,), (cb,)), ((), ())), preferred_element_type=F32)


def stat_rows(m, l):
    m1 = m.astype(BF16).astype(F32)
    r = m - m1
    m2 = r.astype(BF16).astype(F32)
    m3 = r - m2
    l1 = l.astype(BF16).astype(F32)
    r = l - l1
    l2 = r.astype(BF16).astype(F32)
    l3 = r - l2
    row = lax.broadcasted_iota(jnp.int32, (16, CHUNK), 0)
    out = jnp.zeros((16, CHUNK), F32)
    for k, part in enumerate((m1, m2, m3, l1, l2, l3)):
        out = jnp.where(row == k, jnp.broadcast_to(part, (16, CHUNK)), out)
    return out.astype(BF16)


def read_stats(tile):
    t = tile.astype(F32)
    m = (t[0:1] + t[1:2]) + t[2:3]
    l = (t[3:4] + t[4:5]) + t[5:6]
    return m, l


def kernel(
    q_hbm, pk_hbm, pv_hbm, st_hbm, kw_hbm, vw_hbm, sk_hbm, sv_hbm, len_hbm, asg_hbm, ow_hbm, rot_hbm,
    proj_ref, kv_ref,
    st_v, w_v, q_v, k_v, v_v, vt_v, ow_v, rot_v, len_v, asg_v,
    key_send, key_recv, val_send, val_recv, keyz_send, keyz_recv, valz_send, valz_recv, valz_kept,
    acc_v, m_v, l_v,
    low_send, low_recv, high_send, high_recv, lowz_send, lowz_recv, highz_send, highz_recv,
    ag_v, part_v, out_send, out_recv,
    lsem, wsem, s1, r1, s2, r2, s3, r3, s4, r4, s5, r5, s6, r6, s7, r7, s8, r8, s9, r9, s10, r10, s11, r11,
):
    c = lax.axis_index("ctx")
    h = lax.axis_index("head")
    p = lax.axis_index("pool")
    y = c // NX
    x = c % NX

    def plane_peer(i):
        return ((y + i // NX) % NX) * NX + (x + i % NX) % NX

    def remote(src, dst, ss, rs, cc, hh, pp):
        return pltpu.make_async_remote_copy(
            src_ref=src, dst_ref=dst, send_sem=ss, recv_sem=rs,
            device_id={"ctx": cc, "head": hh, "pool": pp},
            device_id_type=pl.DeviceIdType.MESH,
        )

    shard = c * POOL + p
    loads = [
        pltpu.make_async_copy(st_hbm, st_v, lsem.at[0]),
        pltpu.make_async_copy(kw_hbm, w_v.at[:, pl.ds(0, HD)], lsem.at[1]),
        pltpu.make_async_copy(vw_hbm, w_v.at[:, pl.ds(HD, HD)], lsem.at[2]),
        pltpu.make_async_copy(q_hbm, q_v, lsem.at[3]),
        pltpu.make_async_copy(pk_hbm, k_v.at[pl.ds(0, CACHED)], lsem.at[4]),
        pltpu.make_async_copy(sk_hbm, k_v.at[pl.ds(CACHED, SUFFIX)], lsem.at[5]),
        pltpu.make_async_copy(pv_hbm, v_v.at[pl.ds(0, CACHED)], lsem.at[6]),
        pltpu.make_async_copy(sv_hbm, v_v.at[pl.ds(CACHED, SUFFIX)], lsem.at[7]),
        pltpu.make_async_copy(rot_hbm.at[c], rot_v, lsem.at[8]),
        pltpu.make_async_copy(len_hbm, len_v, lsem.at[9]),
        pltpu.make_async_copy(asg_hbm, asg_v, lsem.at[10]),
    ]
    weights = [
        pltpu.make_async_copy(ow_hbm.at[:, f], ow_v.at[f], wsem.at[f]) for f in range(2)
    ]
    for copy in loads[:3]:
        copy.start()

    barrier = pltpu.get_barrier_semaphore()

    def greet(cc, hh, pp):
        pl.semaphore_signal(
            barrier, inc=1, device_id={"ctx": cc, "head": hh, "pool": pp},
            device_id_type=pl.DeviceIdType.MESH,
        )

    for i in FARTHEST:
        greet(plane_peer(i), h, p)
    greet(c, h, 1 - p)
    for j in range(1, HEADS):
        greet(c, (h + j) % HEADS, p)

    for copy in loads[:3]:
        copy.wait()

    for k in range(NX):
        rows = pl.ds(k * NX * NEW_CHIP, NX * NEW_CHIP)
        part = jnp.dot(st_v[rows, :], w_v[...], preferred_element_type=F32).astype(BF16)
        key_send[k * NX:(k + 1) * NX] = part[:, :HD].reshape(NX, NEW_CHIP, HD)
        val_send[k * NX:(k + 1) * NX] = part[:, HD:].reshape(NX, NEW_CHIP, HD)
    pl.semaphore_wait(barrier, (PLANE - 1) + 1 + (HEADS - 1))
    for i in FARTHEST:
        cc = plane_peer(i)
        remote(key_send.at[cc], key_recv.at[i], s1.at[i], r1.at[i], cc, h, p).start()
    for copy in loads[3:]:
        copy.start()

    for copy in weights:
        copy.start()

    def drain(src, dst, ss, rs):
        def left(i, carry):
            remote(src.at[c], dst.at[i], ss.at[i], rs.at[i], c, h, p).wait_send()
            return carry

        lax.fori_loop(1, PLANE, left, 0)

    for copy in loads[3:8] + loads[9:]:
        copy.wait()
    vt_v[...] = v_v[...].astype(F32).T.astype(BF16)
    suffix_id = shard
    lim = jnp.where(asg_v[...] == suffix_id, len_v[0], 0).astype(BF16)
    lim = jnp.broadcast_to(lim, (16, 256))

    def cached_block(b, carry):
        who = lax.broadcasted_iota(jnp.int32, (256, 256), 0)
        row = lax.broadcasted_iota(jnp.int32, (256, 256), 1)
        spread = jnp.where(who == b * 32 + row // GROUP, 1.0, 0.0).astype(BF16)
        lim_rows = mm(lim, spread, 1, 0)[0:1]
        qb = q_v[pl.ds(pl.multiple_of(b * 256, 256), 256), :]
        s = mm(k_v[...], qb, 1, 1) * SCALE
        key = lax.broadcasted_iota(jnp.int32, (SUFFIX, 256), 0).astype(F32)
        side = jnp.where(key < lim_rows, s[CACHED:], -jnp.inf)
        m = jnp.maximum(
            jnp.max(s[:CACHED], 0, keepdims=True), jnp.max(side, 0, keepdims=True)
        )
        main_e = jnp.exp2(s[:CACHED] - m)
        side_e = jnp.exp2(side - m)
        l = jnp.sum(main_e, 0, keepdims=True) + jnp.sum(side_e, 0, keepdims=True)
        e = jnp.concatenate([main_e.astype(BF16), side_e.astype(BF16)], 0)
        o = mm(vt_v[...], e, 1, 0)
        for k in range(2):
            lanes = slice(k * CHUNK, (k + 1) * CHUNK)
            acc_v[b * 2 + k] = o[:, lanes]
            m_v[b * 2 + k] = jnp.broadcast_to(m[:, lanes], (8, CHUNK))
            l_v[b * 2 + k] = jnp.broadcast_to(l[:, lanes], (8, CHUNK))
        return carry

    lax.fori_loop(0, 6, cached_block, 0, unroll=3)
    for i in FARTHEST:
        cc = plane_peer(i)
        remote(val_send.at[cc], val_recv.at[i], s7.at[i], r7.at[i], cc, h, p).start()
    lax.fori_loop(6, 8, cached_block, 0, unroll=2)

    mine = jnp.dot(
        st_v[pl.ds(pl.multiple_of(c * NEW_CHIP, NEW_CHIP), NEW_CHIP), :], w_v[...],
        preferred_element_type=F32,
    )

    def sum_keys(i, acc):
        remote(key_send.at[c], key_recv.at[i], s1.at[i], r1.at[i], c, h, p).wait_recv()
        return acc + key_recv[i].astype(F32)

    keyz_send[...] = lax.fori_loop(1, PLANE, sum_keys, mine[:, :HD])
    swap = remote(keyz_send, keyz_recv, s2, r2, c, h, 1 - p)
    swap.start()
    drain(key_send, key_recv, s1, r1)

    def sum_values(i, acc):
        remote(val_send.at[c], val_recv.at[i], s7.at[i], r7.at[i], c, h, p).wait_recv()
        return acc + val_recv[i].astype(F32)

    values = lax.fori_loop(1, PLANE, sum_values, mine[:, HD:])
    first = p == 0
    new_vt = values.T.astype(BF16)
    loads[8].wait()
    swap.wait_recv()
    raw = keyz_send[...] + keyz_recv[...]
    turned = pltpu.roll(raw, HD // 2, 1)
    new_k = (raw * rot_v[:, :HD] + turned * rot_v[:, HD:]).astype(BF16)
    token = lax.broadcasted_iota(jnp.int32, (NEW_CHIP, CHUNK), 0)
    counted = jnp.where((token // NEW_DEV) == p, 1.0, 0.0).astype(F32)

    def new_block(dy):
        yy = (y + dy) % NX
        qb = q_v[pl.ds(pl.multiple_of(yy * 512, 512), 512), :]
        s = mm(new_k, qb, 1, 1) * SCALE
        s_max = jnp.max(s, 0, keepdims=True)
        for k in range(NX):
            lanes = slice(k * CHUNK, (k + 1) * CHUNK)
            cc = yy * NX + k
            m_old = m_v[cc][0:1]
            m_new = jnp.maximum(m_old, s_max[:, lanes])
            shrink = jnp.exp2(m_old - m_new)
            e = jnp.exp2(s[:, lanes] - m_new)
            l_new = l_v[cc][0:1] * shrink + jnp.sum(e * counted, 0, keepdims=True)
            o = acc_v[cc] * shrink + mm(new_vt, e.astype(BF16), 1, 0)
            low_send[cc, 0:HALF] = o[:HALF].astype(BF16)
            low_send[cc, HALF:FIRST] = stat_rows(m_new, l_new)
            high_send[cc] = o[HALF:].astype(BF16)
            if dy == 0:
                acc_v[cc] = o
                m_v[cc] = jnp.broadcast_to(m_new, (8, CHUNK))
                l_v[cc] = jnp.broadcast_to(l_new, (8, CHUNK))

    for dy in (2, 1, 3, 0):
        new_block(dy)

        for dx in (2, 1, 3, 0):
            i = dy * NX + dx
            if i > 0:
                cc = plane_peer(i)
                remote(low_send.at[cc], low_recv.at[i], s3.at[i], r3.at[i], cc, h, p).start()
    for i in FARTHEST:
        cc = plane_peer(i)
        remote(low_send.at[cc], low_recv.at[i], s3.at[i], r3.at[i], cc, h, p).wait_send()
        remote(high_send.at[cc], high_recv.at[i], s9.at[i], r9.at[i], cc, h, p).start()

    kv_ref[0] = jnp.where(first, new_k[:NEW_DEV], new_k[NEW_DEV:])
    valz_send[...] = jnp.where(first, values[NEW_DEV:], values[:NEW_DEV]).astype(BF16)
    valz_kept[...] = jnp.where(first, values[:NEW_DEV], values[NEW_DEV:])
    swap_values = remote(valz_send, valz_recv, s8, r8, c, h, 1 - p)
    swap_values.start()
    drain(val_send, val_recv, s7, r7)
    swap.wait_send()

    def sum_low(i, state):
        remote(low_send.at[c], low_recv.at[i], s3.at[i], r3.at[i], c, h, p).wait_recv()
        acc, m, l = state
        m_in, l_in = read_stats(low_recv[i, HALF:FIRST])
        m_all = jnp.maximum(m, m_in)
        a = jnp.exp2(m - m_all)
        b = jnp.exp2(m_in - m_all)
        return (acc * a + low_recv[i, 0:HALF].astype(F32) * b, m_all, l * a + l_in * b)

    own_m = m_v[c][0:1]
    low, m, l = lax.fori_loop(1, PLANE, sum_low, (acc_v[c, 0:HALF], own_m, l_v[c][0:1]))
    lowz_send[0:HALF] = low.astype(BF16)
    lowz_send[HALF:FIRST] = stat_rows(m, l)
    swap_low = remote(lowz_send, lowz_recv, s4, r4, c, h, 1 - p)
    swap_low.start()

    def sum_high(i, acc):
        remote(high_send.at[c], high_recv.at[i], s9.at[i], r9.at[i], c, h, p).wait_recv()
        m_in, _ = read_stats(low_recv[i, HALF:FIRST])
        return acc + high_recv[i].astype(F32) * jnp.exp2(m_in - m)

    high = lax.fori_loop(1, PLANE, sum_high, acc_v[c, HALF:HD] * jnp.exp2(own_m - m))
    highz_send[...] = high.astype(BF16)
    swap_high = remote(highz_send, highz_recv, s10, r10, c, h, 1 - p)
    swap_high.start()

    to = lax.broadcasted_iota(jnp.int32, (HALF, CHUNK), 0)
    frm = lax.broadcasted_iota(jnp.int32, (HALF, CHUNK), 1)
    perms = [
        jnp.where(frm == (to % 16) * GROUP + (to // 16) * 2 + k, 1.0, 0.0).astype(BF16)
        for k in range(2)
    ]
    drain(high_send, high_recv, s9, r9)

    swap_low.wait_recv()
    m_in, l_in = read_stats(lowz_recv[HALF:FIRST])
    m_all = jnp.maximum(m, m_in)
    a = jnp.exp2(m - m_all)
    b = jnp.exp2(m_in - m_all)
    inverse = 1.0 / (l * a + l_in * b)
    a, b = a * inverse, b * inverse

    def share(f, mine, other, ss, rs):
        att = (mine * a + other.astype(F32) * b).astype(BF16)
        ag_v[f, c] = jnp.concatenate([mm(perm, att, 1, 1) for perm in perms], 1).astype(BF16)
        for i in FARTHEST:
            remote(ag_v.at[f, c], ag_v.at[f, c], ss.at[i], rs.at[i], plane_peer(i), h, p).start()

    share(0, low, lowz_recv[0:HALF], s5, r5)
    swap_high.wait_recv()
    share(1, high, highz_recv[...], s11, r11)
    swap_values.wait_recv()
    kv_ref[1] = (valz_kept[...] + valz_recv[...].astype(F32)).astype(BF16)
    swap_values.wait_send()
    swap_low.wait_send()
    swap_high.wait_send()
    for copy in weights:
        copy.wait()

    def product(f, yy, dy, ss, rs):
        for dx in range(NX):
            i = dy * NX + dx
            if i > 0:
                src = yy * NX + (x + NX - dx) % NX
                remote(ag_v.at[f, c], ag_v.at[f, src], ss.at[i], rs.at[i], c, h, p).wait_recv()
        rows = ag_v[f, pl.ds(yy * NX, NX)]
        rows = jnp.concatenate(
            [rows[:, k * 16:(k + 1) * 16, :].reshape(NX * 16, HD) for k in range(GROUP // 2)], 1
        )
        return jnp.dot(rows, ow_v[f].reshape(GROUP * HALF, OUT_COLS), preferred_element_type=F32)

    for dy in (0, 1, 3, 2):
        yy = (y + NX - dy) % NX
        part_v[pl.ds(yy * 2, 2)] = product(0, yy, dy, s5, r5).reshape(2, 32, OUT_COLS)
    for dy in (0, 1, 3, 2):
        yy = (y + NX - dy) % NX
        out = part_v[pl.ds(yy * 2, 2)].reshape(NX * 16, OUT_COLS) + product(1, yy, dy, s11, r11)
        part_v[pl.ds(yy * 2, 2)] = out.reshape(2, 32, OUT_COLS)
        out_send[pl.ds(yy * 2, 2)] = out.astype(BF16).reshape(2, 32, OUT_COLS)
        for k in range(2):
            hh = yy * 2 + k
            j = (hh + HEADS - h) % HEADS

            @pl.when(j != 0)
            def _():
                remote(out_send.at[hh], out_recv.at[j], s6.at[j], r6.at[j], c, hh, p).start()

    def left_ag(i, carry):
        remote(ag_v.at[0, c], ag_v.at[0, c], s5.at[i], r5.at[i], c, h, p).wait_send()
        remote(ag_v.at[1, c], ag_v.at[1, c], s11.at[i], r11.at[i], c, h, p).wait_send()
        return carry

    lax.fori_loop(1, PLANE, left_ag, 0)

    def sum_out(j, acc):
        remote(out_send.at[h], out_recv.at[j], s6.at[j], r6.at[j], c, h, p).wait_recv()
        return acc + out_recv[j].astype(F32)

    proj_ref[...] = lax.fori_loop(1, HEADS, sum_out, part_v[h], unroll=True).astype(BF16)

    def left_out(j, carry):
        remote(out_send.at[h], out_recv.at[j], s6.at[j], r6.at[j], c, h, p).wait_send()
        return carry

    lax.fori_loop(1, HEADS, left_out, 0)


def body(
    queries, prefix_keys, prefix_values, new_states, key_weight, value_weight,
    suffix_keys, suffix_values, suffix_lengths, assignment, out_weight,
):
    rot = jnp.asarray(rotary_tables())
    hbm = pl.BlockSpec(memory_space=pl.ANY)
    vmem = pl.BlockSpec(memory_space=pltpu.VMEM)
    dma = pltpu.SemaphoreType.DMA
    projected, new_both = pl.pallas_call(
        kernel,
        out_shape=(
            jax.ShapeDtypeStruct((32, OUT_COLS), BF16),
            jax.ShapeDtypeStruct((2, NEW_DEV, HD), BF16),
        ),
        in_specs=[hbm] * 12,
        out_specs=(vmem, vmem),
        scratch_shapes=[
            pltpu.VMEM((NEW, FEAT), BF16),
            pltpu.VMEM((FEAT, 2 * HD), BF16),
            pltpu.VMEM((ROWS, HD), BF16),
            pltpu.VMEM((CACHED + SUFFIX, HD), BF16),
            pltpu.VMEM((CACHED + SUFFIX, HD), BF16),
            pltpu.VMEM((HD, CACHED + SUFFIX), BF16),
            pltpu.VMEM((2, GROUP, HALF, OUT_COLS), BF16),
            pltpu.VMEM((NEW_CHIP, 2 * HD), F32),
            pltpu.SMEM((1,), jnp.int32),
            pltpu.VMEM((1, 256), jnp.int32),
            pltpu.VMEM((PLANE, NEW_CHIP, HD), BF16),
            pltpu.VMEM((PLANE, NEW_CHIP, HD), BF16),
            pltpu.VMEM((PLANE, NEW_CHIP, HD), BF16),
            pltpu.VMEM((PLANE, NEW_CHIP, HD), BF16),
            pltpu.VMEM((NEW_CHIP, HD), F32),
            pltpu.VMEM((NEW_CHIP, HD), F32),
            pltpu.VMEM((NEW_DEV, HD), BF16),
            pltpu.VMEM((NEW_DEV, HD), BF16),
            pltpu.VMEM((NEW_DEV, HD), F32),
            pltpu.VMEM((PLANE, HD, CHUNK), F32),
            pltpu.VMEM((PLANE, 8, CHUNK), F32),
            pltpu.VMEM((PLANE, 8, CHUNK), F32),
            pltpu.VMEM((PLANE, FIRST, CHUNK), BF16),
            pltpu.VMEM((PLANE, FIRST, CHUNK), BF16),
            pltpu.VMEM((PLANE, HALF, CHUNK), BF16),
            pltpu.VMEM((PLANE, HALF, CHUNK), BF16),
            pltpu.VMEM((FIRST, CHUNK), BF16),
            pltpu.VMEM((FIRST, CHUNK), BF16),
            pltpu.VMEM((HALF, CHUNK), BF16),
            pltpu.VMEM((HALF, CHUNK), BF16),
            pltpu.VMEM((2, PLANE, HALF, HD), BF16),
            pltpu.VMEM((HEADS, 32, OUT_COLS), F32),
            pltpu.VMEM((HEADS, 32, OUT_COLS), BF16),
            pltpu.VMEM((HEADS, 32, OUT_COLS), BF16),
            dma((11,)),
            dma((2,)),
            dma((PLANE,)), dma((PLANE,)),
            dma, dma,
            dma((PLANE,)), dma((PLANE,)),
            dma, dma,
            dma((PLANE,)), dma((PLANE,)),
            dma((HEADS,)), dma((HEADS,)),
            dma((PLANE,)), dma((PLANE,)),
            dma, dma,
            dma((PLANE,)), dma((PLANE,)),
            dma, dma,
            dma((PLANE,)), dma((PLANE,)),
        ],
        compiler_params=pltpu.CompilerParams(
            collective_id=0, has_side_effects=True, vmem_limit_bytes=55168 * 1024
        ),
    )(
        queries.reshape(ROWS, HD),
        prefix_keys.reshape(CACHED, HD),
        prefix_values.reshape(CACHED, HD),
        new_states,
        key_weight,
        value_weight,
        suffix_keys.reshape(SUFFIX, HD),
        suffix_values.reshape(SUFFIX, HD),
        suffix_lengths,
        assignment.reshape(1, 256),
        out_weight.reshape(GROUP, 2, HALF, OUT_COLS),
        rot,
    )
    return (
        projected,
        new_both[0].reshape(NEW_DEV, 1, HD),
        new_both[1].reshape(NEW_DEV, 1, HD),
    )


def solution(mesh):
    in_specs = (
        P(None, "head", None),
        P(("ctx", "pool"), "head", None),
        P(("ctx", "pool"), "head", None),
        P(None, ("ctx", "pool")),
        P(("ctx", "pool"), "head"),
        P(("ctx", "pool"), "head"),
        P(("ctx", "pool"), None, "head", None),
        P(("ctx", "pool"), None, "head", None),
        P(("ctx", "pool")),
        P(),
        P("head", ("ctx", "pool")),
    )
    out_specs = (
        P("head", ("ctx", "pool")),
        P(("ctx", "pool"), "head", None),
        P(("ctx", "pool"), "head", None),
    )
    return jax.shard_map(body, mesh=mesh, in_specs=in_specs, out_specs=out_specs, check_vma=False)
```
